128 devices in a mesh: expert: 16 (over y, x), tensor: 8 (over z, core).
Axes of the slice: x: 4, y: 4, z: 4, core: 2. Of those that a mesh axis runs over, the one named last changes fastest.
Arguments:
- tokens: bfloat16 [2048, 4096], P('expert'), may hold values from -6 to 6
- expert_ids: int32 [2048, 8], P('expert'), may hold values from 0 to 15, all different within a row; in each aligned block of 128 rows (0 to 127, 128 to 255, ...) at most 72 rows name the same one
- gate_probs: float32 [2048, 8], P('expert'), may hold values from 0.03 to 0.5
- grad_out: bfloat16 [2048, 4096], P('expert'), may hold values from -6 to 6
- gate_up: bfloat16 [16, 2, 1536, 4096], P('expert', None, 'tensor'), may hold values from -0.09375 to 0.09375
- down_proj: bfloat16 [16, 1536, 4096], P('expert', 'tensor'), may hold values from -0.15625 to 0.15625
Outputs:
- mixed: bfloat16 [2048, 4096], P('expert', 'tensor')
- grad_tokens: bfloat16 [2048, 4096], P('expert', 'tensor')
- grad_gate_up: bfloat16 [16, 2, 1536, 4096], P('expert', None, 'tensor')
- grad_down: bfloat16 [16, 1536, 4096], P('expert', 'tensor')
The draws below stay inside these ranges and needn't reach their ends.
Inputs may be any that keep to these rules, and one draw needn't show every extreme that they name: `expert_ids`: each token names 8 different experts. Among the 128 tokens of one index of the expert axis no expert is named by more than 72 tokens, a bound that some block reaches.
All inputs are finite; a program needn't handle non-finite values.
Results may differ from the reference program's by a relative error of at most 0.019.
Values may be sent and summed in bfloat16 or wider, within the bound.
No kernel may reach another device: no remote copies, remote signals or barrier semaphores. Data moves between devices by JAX's collectives and lax.ppermute only.
A program may use at most 192 MiB of HBM per device.

```python
import math
import jax
import jax.numpy as jnp
import numpy as np
from jax import lax

D = 4096
FF = 1536
TOPK = 8
EXPERTS = 16
TOK_DEV = 128
CAP = 72
TOKENS = 2048
N_EXPERT = 16
N_TENSOR = 8


def level_of(own_key, shape, shards, smallest, top_value):
    factor_of = 1.0
    for position, parts in shards:
        draws = jax.random.uniform(jax.random.fold_in(jax.random.fold_in(own_key, 6), position), (parts,), jnp.float32, smallest / len(shards), top_value / len(shards))
        factor_of = factor_of * jnp.repeat(jnp.exp(draws), shape[position] // parts).reshape((-1,) + (1,) * (len(shape) - 1 - position))
    return factor_of


def deal_out(rng, own, number, rows, count, top, bound, slope):
    sequence = jax.random.permutation(rng, count)
    crowded, usual = shares(count, rows * top, bound, slope, True), shares(count, rows * top, bound, slope, False)
    places = jnp.arange(count)

    def named(lengths, offset_by):
        used = int((lengths > 0).sum())
        fixed = max(1, used // 4)
        shifted = fixed + (places - fixed + offset_by * (used - fixed)) % max(1, count - fixed)
        return jnp.zeros((count,), jnp.int32).at[sequence[jnp.where(places < fixed, places, shifted)]].set(jnp.asarray(lengths, jnp.int32))

    lengths = jnp.where(number % 4 == 0, named(crowded, number // 4), named(usual, number - number // 4 - 1))
    mixed = jax.random.permutation(jax.random.fold_in(own, 3), count)
    giver, sink = mixed[0:count // 2 * 2:2], mixed[1:count // 2 * 2:2]
    room = jnp.minimum(lengths[giver] - 1, bound - lengths[sink]) // 2
    room = jnp.where((giver == sequence[0]) | (sink == sequence[0]) | (lengths[sink] == 0), 0, jnp.maximum(room, 0))
    shifted = jax.random.randint(jax.random.fold_in(own, 4), (count // 2,), 0, 1 << 20) % (room + 1)
    lengths = lengths.at[giver].add(-shifted).at[sink].add(shifted)
    members = jnp.searchsorted(jnp.cumsum(lengths), jnp.arange(rows * top), side="right").astype(jnp.int32)
    listing = members.reshape(top, rows).T
    listing = listing[jax.random.permutation(jax.random.fold_in(own, 1), rows)]
    offset_by = jax.random.randint(jax.random.fold_in(own, 2), (rows, 1), 0, top)
    return jnp.take_along_axis(listing, (jnp.arange(top)[None, :] + offset_by) % top, axis=1)


def shares(number_of, total, limit, skew, full):
    portions = [(1 << 20) // math.isqrt(grade ** skew) + 1 for grade in range(1, number_of + 1)]
    largest = limit if full else min(limit, max(-(-total // number_of), total * portions[0] // sum(portions)))
    least = 1 if total - largest >= number_of - 1 else 0
    counts, rest = [largest] + [least] * (number_of - 1), total - largest - least * (number_of - 1)
    while rest > 0:
        free = [i for i in range(1, number_of) if counts[i] < largest] or [i for i in range(1, number_of) if counts[i] < limit]
        mass, remaining = sum([portions[i] for i in free]), rest
        for i in free:
            extra = min(limit - counts[i], max(1, remaining * portions[i] // mass), rest)
            counts[i] = counts[i] + extra
            rest = rest - extra
    return np.array(counts)


def centred(key, dims, spread, bound, pieces=(), held_as=jnp.bfloat16):
    loudness = level_of(key, dims, pieces, -0.22, 0.18) if pieces else 1.0
    entries = jax.random.normal(key, dims, jnp.float32) * spread * loudness
    return jnp.minimum(jnp.maximum(entries, -bound), bound).astype(held_as)


def setup_inputs(seed: int = 0) -> dict:
    keys = jax.random.split(jax.random.key(seed), 7)
    tokens = centred(keys[0], (TOKENS, D), 1.0, 6.0, ((0, 16),))
    expert_ids_keys = jax.random.split(jax.random.fold_in(keys[1], 1), TOKENS // TOK_DEV)
    expert_ids_turns = jax.random.permutation(jax.random.fold_in(keys[1], 3), TOKENS // TOK_DEV)
    expert_ids = jax.vmap(lambda own, number: deal_out(jax.random.fold_in(keys[1], 2), own, number, TOK_DEV, EXPERTS, TOPK, CAP, 1))(expert_ids_keys, expert_ids_turns).reshape((TOKENS, TOPK))
    gate_probs = jnp.clip(jnp.exp(math.log(0.5) - 2.8134107 * jax.random.uniform(keys[2], (TOKENS, TOPK), jnp.float32) ** level_of(keys[2], (TOKENS, TOPK), ((0, 16),), -0.2, 0.2)), 0.03, 0.5)
    grad_out = centred(keys[3], (TOKENS, D), 1.0, 6.0, ((0, 16),))
    gate_up = centred(keys[4], (EXPERTS, 2, FF, D), D ** -0.5, 0.09375, ((0, 16), (2, 8)))
    down_proj = centred(keys[5], (EXPERTS, FF, D), FF ** -0.5, 0.15625, ((0, 16), (1, 8)))
    return {"tokens": tokens, "expert_ids": expert_ids, "gate_probs": gate_probs, "grad_out": grad_out, "gate_up": gate_up, "down_proj": down_proj}


def reference(tokens, expert_ids, gate_probs, grad_out, gate_up, down_proj):
    model_width = tokens.shape[1]
    block_units = FF // N_TENSOR
    capacity_rows = N_EXPERT * CAP

    def expert_step(carry, expert):
        out_acc, grad_acc = carry
        w_gate_up = gate_up[expert].reshape(2 * FF, model_width)
        w_down = down_proj[expert]
        hits = expert_ids == expert
        chosen = jnp.any(hits, axis=1).astype(jnp.int32)
        weight_tok = jnp.sum(jnp.where(hits, gate_probs, 0.0), axis=1)
        order = jnp.argsort(1 - chosen, stable=True)[:capacity_rows].astype(jnp.int32)
        valid = chosen[order] > 0
        inputs = jnp.where(valid[:, None], tokens[order], jnp.zeros((), tokens.dtype))
        row_weight = jnp.where(valid, weight_tok[order], 0.0)
        gated = jnp.dot(inputs, w_gate_up.T, preferred_element_type=jnp.float32)
        gated = gated.reshape(capacity_rows, 2, FF)
        gate = gated[:, 0]
        upval = gated[:, 1]
        sig = jax.nn.sigmoid(gate)
        hidden = (gate * sig * upval).astype(jnp.bfloat16)
        partial_value = jnp.einsum("rsf,sfd->rsd",
                             hidden.reshape(capacity_rows, N_TENSOR, block_units).astype(jnp.float32),
                             w_down.reshape(N_TENSOR, block_units, model_width).astype(jnp.float32))
        expert_out = jnp.sum(lax.optimization_barrier(partial_value.astype(jnp.bfloat16)).astype(jnp.float32), axis=1)
        out_acc = out_acc.at[order].add(expert_out * row_weight[:, None])
        cot = jnp.where(valid[:, None], row_weight[:, None] * grad_out[order], 0.0).astype(jnp.bfloat16)
        dhid = jnp.dot(cot, w_down.T, preferred_element_type=jnp.float32)
        grad_down_e = jnp.dot(hidden.T, cot, preferred_element_type=jnp.float32).astype(jnp.bfloat16)
        dgate = dhid * upval * sig * (1.0 + gate * (1.0 - sig))
        dup = dhid * gate * sig
        dgu = jnp.stack([dgate, dup], axis=1).astype(jnp.bfloat16)
        grad_gu_e = jnp.dot(dgu.reshape(capacity_rows, 2 * FF).T, inputs, preferred_element_type=jnp.float32)
        grad_gu_e = grad_gu_e.reshape(2, FF, model_width).astype(jnp.bfloat16)
        back = jnp.einsum("rcsf,csfd->rsd",
                          dgu.reshape(capacity_rows, 2, N_TENSOR, block_units).astype(jnp.float32),
                          w_gate_up.reshape(2, N_TENSOR, block_units, model_width).astype(jnp.float32))
        grad_in = jnp.sum(lax.optimization_barrier(back.astype(jnp.bfloat16)).astype(jnp.float32), axis=1)
        grad_acc = grad_acc.at[order].add(jnp.where(valid[:, None], grad_in, 0.0))
        return (out_acc, grad_acc), (grad_gu_e, grad_down_e)

    start = (jnp.zeros(tokens.shape, jnp.float32), jnp.zeros(tokens.shape, jnp.float32))
    (out_acc, grad_acc), (grad_gate_up, grad_down) = lax.scan(expert_step, start, jnp.arange(EXPERTS, dtype=jnp.int32))
    return out_acc.astype(jnp.bfloat16), grad_acc.astype(jnp.bfloat16), grad_gate_up, grad_down
```

```python
import jax
import jax.numpy as jnp
from jax import lax
from jax.experimental import pallas as pl
from jax.experimental.pallas import tpu as pltpu
from jax.sharding import PartitionSpec as P

EXPERTS = 16
CAP = 72
GROUPS = 16
TOK = 128
D = 4096
UNITS = 192
TENSOR = 8
SHARE = D // TENSOR
STEP_GROUPS = 4
PAIRS = STEP_GROUPS // 2
ROWS = STEP_GROUPS * CAP
STEPS = GROUPS // STEP_GROUPS
ALL_ROWS = GROUPS * CAP
F32 = jnp.float32
BF16 = jnp.bfloat16
VMEM_LIMIT = 56 * 1024 * 1024


def nt(a, b):
    return lax.dot_general(a, b, (((1,), (1,)), ((), ())), preferred_element_type=F32)


def nn(a, b):
    return lax.dot_general(a, b, (((1,), (0,)), ((), ())), preferred_element_type=F32)


def forward_kernel(x_ref, row_ref, wgu_ref, wd_ref, in_ref, gate_ref, up_ref, hid_ref, out_ref):
    for j in range(PAIRS):
        x = x_ref[2 * j : 2 * j + 2].reshape(2 * TOK, D)
        hit = lax.broadcasted_iota(jnp.int32, (2 * CAP, 2 * TOK), 0) == row_ref[j]
        onehot = jnp.where(hit, 1.0, 0.0).astype(BF16)
        in_ref[2 * CAP * j : 2 * CAP * (j + 1), :] = nn(onehot, x).astype(BF16)
    rows = in_ref[...]
    gate = nt(rows, wgu_ref[0])
    up = nt(rows, wgu_ref[1])
    gate_ref[...] = gate
    up_ref[...] = up
    hidden = (gate * jax.nn.sigmoid(gate) * up).astype(BF16)
    hid_ref[...] = hidden
    for c in range(TENSOR):
        cols = slice(SHARE * c, SHARE * (c + 1))
        out_ref[c] = nn(hidden, wd_ref[:, cols]).astype(BF16)


def backward_kernel(g_ref, row_ref, w_ref, gate_ref, up_ref, wgu_ref, wd_ref, cot_ref, dgu_ref, back_ref):
    for j in range(PAIRS):
        g = g_ref[2 * j : 2 * j + 2].reshape(2 * TOK, D)
        hit = lax.broadcasted_iota(jnp.int32, (2 * CAP, 2 * TOK), 0) == row_ref[j]
        onehot = jnp.where(hit, 1.0, 0.0).astype(BF16)
        weight = jnp.sum(jnp.where(hit, w_ref[j], 0.0), axis=1, keepdims=True)
        cot_ref[2 * CAP * j : 2 * CAP * (j + 1), :] = (nn(onehot, g) * weight).astype(BF16)
    dhid = nt(cot_ref[...], wd_ref[...])
    gate = gate_ref[...]
    up = up_ref[...]
    sig = jax.nn.sigmoid(gate)
    dgate = (dhid * up * sig * (1.0 + gate * (1.0 - sig))).astype(BF16)
    dup = (dhid * gate * sig).astype(BF16)
    dgu_ref[0] = dgate
    dgu_ref[1] = dup
    for c in range(TENSOR):
        cols = slice(SHARE * c, SHARE * (c + 1))
        back_ref[c] = (nn(dgate, wgu_ref[0, :, cols]) + nn(dup, wgu_ref[1, :, cols])).astype(BF16)


def combine_kernel(weighted, r_ref, w_ref, o_ref):
    w = w_ref[...]
    mask = w > 0.0
    ones = jnp.where(mask, 1.0, 0.0)
    lower = lax.broadcasted_iota(jnp.int32, (TOK, TOK), 1) < lax.broadcasted_iota(jnp.int32, (TOK, TOK), 0)
    slot = nn(jnp.where(lower, 1.0, 0.0).astype(BF16), ones.astype(BF16))
    slot = jnp.where(mask, slot, -1.0).astype(jnp.int32)
    scale = w if weighted else ones
    total = jnp.zeros(o_ref.shape, F32)
    for e in range(EXPERTS):
        hit = lax.broadcasted_iota(jnp.int32, (TOK, CAP), 1) == slot[:, e : e + 1]
        onehot = jnp.where(hit, 1.0, 0.0).astype(BF16)
        total += nn(onehot, r_ref[e]) * scale[:, e : e + 1]
    o_ref[...] = total.astype(BF16)


def params():
    return pltpu.CompilerParams(vmem_limit_bytes=VMEM_LIMIT, dimension_semantics=("arbitrary",))


def gathered_spec(which):
    return pl.BlockSpec((STEP_GROUPS, TENSOR, None, TOK // TENSOR, D), lambda i: (i, 0, which, 0, 0))


def whole(shape):
    return pl.BlockSpec(shape, lambda i: (0,) * len(shape), pipeline_mode=pl.Buffered(1))


ROW_SPEC = pl.BlockSpec((PAIRS, 1, 2 * TOK), lambda i: (i, 0, 0))
WIDE_SPEC = pl.BlockSpec((ROWS, D), lambda i: (i, 0))
UNIT_SPEC = pl.BlockSpec((ROWS, UNITS), lambda i: (i, 0))
SHARE_SPEC = pl.BlockSpec((TENSOR, ROWS, SHARE), lambda i: (0, i, 0))


def forward(gathered, row_of, wgu, wd):
    return pl.pallas_call(
        forward_kernel,
        grid=(STEPS,),
        in_specs=[gathered_spec(0), ROW_SPEC, whole(wgu.shape), whole(wd.shape)],
        out_specs=[WIDE_SPEC, UNIT_SPEC, UNIT_SPEC, UNIT_SPEC, SHARE_SPEC],
        out_shape=[
            jax.ShapeDtypeStruct((ALL_ROWS, D), BF16),
            jax.ShapeDtypeStruct((ALL_ROWS, UNITS), F32),
            jax.ShapeDtypeStruct((ALL_ROWS, UNITS), F32),
            jax.ShapeDtypeStruct((ALL_ROWS, UNITS), BF16),
            jax.ShapeDtypeStruct((TENSOR, ALL_ROWS, SHARE), BF16),
        ],
        compiler_params=params(),
        cost_estimate=pl.CostEstimate(flops=8_000_000_000, bytes_accessed=42_000_000, transcendentals=221184),
    )(gathered, row_of, wgu, wd)


def backward(gathered, row_of, weight, gate, up, wgu, wd):
    return pl.pallas_call(
        backward_kernel,
        grid=(STEPS,),
        in_specs=[
            gathered_spec(1), ROW_SPEC, ROW_SPEC, UNIT_SPEC, UNIT_SPEC, whole(wgu.shape), whole(wd.shape),
        ],
        out_specs=[
            WIDE_SPEC, pl.BlockSpec((2, ROWS, UNITS), lambda i: (0, i, 0)), SHARE_SPEC,
        ],
        out_shape=[
            jax.ShapeDtypeStruct((ALL_ROWS, D), BF16),
            jax.ShapeDtypeStruct((2, ALL_ROWS, UNITS), BF16),
            jax.ShapeDtypeStruct((TENSOR, ALL_ROWS, SHARE), BF16),
        ],
        compiler_params=params(),
        cost_estimate=pl.CostEstimate(flops=8_000_000_000, bytes_accessed=42_000_000, transcendentals=221184),
    )(gathered, row_of, weight, gate, up, wgu, wd)


def combine(returned, own_weight, weighted):
    return pl.pallas_call(
        lambda *refs: combine_kernel(weighted, *refs),
        out_shape=jax.ShapeDtypeStruct((TOK, returned.shape[2]), BF16),
        compiler_params=pltpu.CompilerParams(vmem_limit_bytes=VMEM_LIMIT),
        cost_estimate=pl.CostEstimate(flops=200_000_000, bytes_accessed=1_400_000, transcendentals=0),
    )(returned, own_weight)


def reduce_and_return(partial_rows):
    summed = lax.psum_scatter(partial_rows, "tensor", scatter_dimension=0, tiled=False)
    return lax.all_to_all(
        summed.reshape(GROUPS, CAP, SHARE), "expert", split_axis=0, concat_axis=0, tiled=True
    )


def on_device(tokens, expert_ids, gate_probs, grad_out, gate_up, down_proj):
    part = TOK // TENSOR
    first = lax.axis_index("tensor") * part
    mine = jnp.concatenate(
        [
            lax.dynamic_slice_in_dim(tokens, first, part, 0),
            lax.dynamic_slice_in_dim(grad_out, first, part, 0),
        ],
        axis=0,
    )
    gathered = lax.all_gather(mine, ("expert", "tensor"), axis=0, tiled=True)
    gathered = gathered.reshape(GROUPS, TENSOR, 2, part, D)

    named = expert_ids[:, :, None] == jnp.arange(EXPERTS, dtype=jnp.int32)
    own_weight = jnp.sum(jnp.where(named, gate_probs[:, :, None], 0.0), axis=1)
    weight = lax.all_to_all(own_weight.T, "expert", split_axis=0, concat_axis=0, tiled=True)
    mask = weight > 0.0
    place = jnp.arange(TOK, dtype=jnp.int32)
    earlier = (place[:, None] < place[None, :]).astype(BF16)
    slot = jnp.dot(mask.astype(BF16), earlier, preferred_element_type=F32).astype(jnp.int32)
    offset = CAP * (jnp.arange(GROUPS, dtype=jnp.int32) % 2)
    row_of = jnp.where(mask, slot + offset[:, None], -1).reshape(GROUPS // 2, 1, 2 * TOK)
    weight = weight.reshape(GROUPS // 2, 1, 2 * TOK)

    wgu, wd = gate_up[0], down_proj[0]
    inputs, gate, up, hidden, partial_out = forward(gathered, row_of, wgu, wd)
    out_back = reduce_and_return(partial_out)
    cot, dgu, partial_back = backward(gathered, row_of, weight, gate, up, wgu, wd)
    grad_back = reduce_and_return(partial_back)
    grad_down = jnp.einsum("rf,rd->fd", hidden, cot, preferred_element_type=F32).astype(BF16)
    grad_gate_up = jnp.einsum("crf,rd->cfd", dgu, inputs, preferred_element_type=F32).astype(BF16)
    mixed = combine(out_back, own_weight, True)
    grad_tokens = combine(grad_back, own_weight, False)
    return (mixed, grad_tokens, grad_gate_up[None], grad_down[None])


def solution(mesh):
    return jax.shard_map(
        on_device,
        mesh=mesh,
        in_specs=(
            P("expert", None),
            P("expert", None),
            P("expert", None),
            P("expert", None),
            P("expert", None, "tensor", None),
            P("expert", "tensor", None),
        ),
        out_specs=(
            P("expert", "tensor"),
            P("expert", "tensor"),
            P("expert", None, "tensor", None),
            P("expert", "tensor", None),
        ),
        check_vma=False,
    )
```

```python
import jax
import jax.numpy as jnp
from jax import lax
from jax.experimental import pallas as pl
from jax.experimental.pallas import tpu as pltpu
from jax.sharding import PartitionSpec as P

EXPERTS = 16
CAP = 72
GROUPS = 16
TOK = 128
D = 4096
UNITS = 192
TENSOR = 8
SHARE = D // TENSOR
HALF = D // 2
DEPTH = TENSOR // 2
STEP_GROUPS = 4
PAIRS = STEP_GROUPS // 2
ROWS = STEP_GROUPS * CAP
STEPS = GROUPS // STEP_GROUPS
ALL_ROWS = GROUPS * CAP
F32 = jnp.float32
BF16 = jnp.bfloat16
VMEM_LIMIT = 56 * 1024 * 1024


def nt(a, b):
    return lax.dot_general(a, b, (((1,), (1,)), ((), ())), preferred_element_type=F32)


def nn(a, b):
    return lax.dot_general(a, b, (((1,), (0,)), ((), ())), preferred_element_type=F32)


def pick_kernel(x_ref, w_ref, o_ref):
    mask = w_ref[...] > 0.0
    earlier = lax.broadcasted_iota(jnp.int32, (TOK, TOK), 0) < lax.broadcasted_iota(jnp.int32, (TOK, TOK), 1)
    ones = jnp.where(mask, 1.0, 0.0).astype(BF16)
    slot = nn(ones, jnp.where(earlier, 1.0, 0.0).astype(BF16))
    slot = jnp.where(mask, slot, -1.0).astype(jnp.int32)
    x = x_ref[...]
    for e in range(EXPERTS):
        hit = lax.broadcasted_iota(jnp.int32, (CAP, TOK), 0) == slot[e : e + 1]
        o_ref[e] = nn(jnp.where(hit, 1.0, 0.0).astype(BF16), x).astype(BF16)


def forward_kernel(
    core_ref, own_ref, other_ref, wgu_ref, wd_ref, in_ref, gate_ref, up_ref, hid_ref, keep_ref, send_ref
):
    core = core_ref[0]
    in_ref[:, pl.ds(pl.multiple_of(core * HALF, HALF), HALF)] = own_ref[...]
    in_ref[:, pl.ds(pl.multiple_of((1 - core) * HALF, HALF), HALF)] = other_ref[...]
    rows = in_ref[...]
    gate = nt(rows, wgu_ref[0])
    up = nt(rows, wgu_ref[1])
    gate_ref[...] = gate
    up_ref[...] = up
    hidden = (gate * jax.nn.sigmoid(gate) * up).astype(BF16)
    hid_ref[...] = hidden
    for ref, parity in ((send_ref, 1 - core), (keep_ref, core)):
        for z in range(DEPTH):
            cols = pl.ds(pl.multiple_of((2 * z + parity) * SHARE, SHARE), SHARE)
            ref[:, SHARE * z : SHARE * (z + 1)] = nn(hidden, wd_ref[:, cols]).astype(BF16)


def backward_kernel(g_ref, row_ref, w_ref, gate_ref, up_ref, wgu_ref, wd_ref, cot_ref, dgu_ref, back_ref):
    for j in range(PAIRS):
        g = g_ref[2 * TOK * j : 2 * TOK * (j + 1), :]
        hit = lax.broadcasted_iota(jnp.int32, (2 * CAP, 2 * TOK), 0) == row_ref[j]
        onehot = jnp.where(hit, 1.0, 0.0).astype(BF16)
        weight = jnp.sum(jnp.where(hit, w_ref[j], 0.0), axis=1, keepdims=True)
        cot_ref[2 * CAP * j : 2 * CAP * (j + 1), :] = (nn(onehot, g) * weight).astype(BF16)
    dhid = nt(cot_ref[...], wd_ref[...])
    gate = gate_ref[...]
    up = up_ref[...]
    sig = jax.nn.sigmoid(gate)
    dgate = (dhid * up * sig * (1.0 + gate * (1.0 - sig))).astype(BF16)
    dup = (dhid * gate * sig).astype(BF16)
    dgu_ref[0] = dgate
    dgu_ref[1] = dup
    for c in range(TENSOR):
        cols = slice(SHARE * c, SHARE * (c + 1))
        back_ref[c] = (nn(dgate, wgu_ref[0, :, cols]) + nn(dup, wgu_ref[1, :, cols])).astype(BF16)


def own_places(w_ref):
    w = w_ref[...]
    mask = w > 0.0
    ones = jnp.where(mask, 1.0, 0.0)
    lower = lax.broadcasted_iota(jnp.int32, (TOK, TOK), 1) < lax.broadcasted_iota(jnp.int32, (TOK, TOK), 0)
    slot = nn(jnp.where(lower, 1.0, 0.0).astype(BF16), ones.astype(BF16))
    return w, ones, jnp.where(mask, slot, -1.0).astype(jnp.int32)


def combine_kernel(r_ref, w_ref, o_ref):
    _, ones, slot = own_places(w_ref)
    total = jnp.zeros(o_ref.shape, F32)
    for e in range(EXPERTS):
        hit = lax.broadcasted_iota(jnp.int32, (TOK, CAP), 1) == slot[:, e : e + 1]
        onehot = jnp.where(hit, 1.0, 0.0).astype(BF16)
        total += nn(onehot, r_ref[e]) * ones[:, e : e + 1]
    o_ref[...] = total.astype(BF16)


def depth_kernel(z_ref, r_ref, w_ref, o_ref):
    w, _, slot = own_places(w_ref)
    total = jnp.zeros((TOK, SHARE), F32)
    for e in range(EXPERTS):
        hit = lax.broadcasted_iota(jnp.int32, (TOK, CAP), 1) == slot[:, e : e + 1]
        onehot = jnp.where(hit, 1.0, 0.0).astype(BF16)
        total += nn(onehot, r_ref[e]) * w[:, e : e + 1]
    o_ref[...] = total.astype(BF16)


def params():
    return pltpu.CompilerParams(vmem_limit_bytes=VMEM_LIMIT, dimension_semantics=("arbitrary",))


def whole(shape):
    return pl.BlockSpec(shape, lambda i: (0,) * len(shape), pipeline_mode=pl.Buffered(1))


ROW_SPEC = pl.BlockSpec((PAIRS, 1, 2 * TOK), lambda i: (i, 0, 0))
WIDE_SPEC = pl.BlockSpec((ROWS, D), lambda i: (i, 0))
UNIT_SPEC = pl.BlockSpec((ROWS, UNITS), lambda i: (i, 0))
SHARE_SPEC = pl.BlockSpec((TENSOR, ROWS, SHARE), lambda i: (0, i, 0))


def pick(x_half, weight_rows):
    return pl.pallas_call(
        pick_kernel,
        out_shape=jax.ShapeDtypeStruct((EXPERTS, CAP, HALF), BF16),
        compiler_params=pltpu.CompilerParams(vmem_limit_bytes=VMEM_LIMIT),
        cost_estimate=pl.CostEstimate(flops=600_000_000, bytes_accessed=5_300_000, transcendentals=0),
    )(x_half, weight_rows)


def forward(core, own, other, wgu, wd):
    wide = pl.BlockSpec((ROWS, D), lambda i, _: (i, 0))
    half = pl.BlockSpec((ROWS, HALF), lambda i, _: (i, 0))
    units = pl.BlockSpec((ROWS, UNITS), lambda i, _: (i, 0))
    once = pl.Buffered(1)
    return pl.pallas_call(
        forward_kernel,
        grid_spec=pltpu.PrefetchScalarGridSpec(
            num_scalar_prefetch=1,
            grid=(STEPS,),
            in_specs=[
                half,
                half,
                pl.BlockSpec(wgu.shape, lambda i, _: (0, 0, 0), pipeline_mode=once),
                pl.BlockSpec(wd.shape, lambda i, _: (0, 0), pipeline_mode=once),
            ],
            out_specs=[wide, units, units, units, half, half],
        ),
        out_shape=[
            jax.ShapeDtypeStruct((ALL_ROWS, D), BF16),
            jax.ShapeDtypeStruct((ALL_ROWS, UNITS), F32),
            jax.ShapeDtypeStruct((ALL_ROWS, UNITS), F32),
            jax.ShapeDtypeStruct((ALL_ROWS, UNITS), BF16),
            jax.ShapeDtypeStruct((ALL_ROWS, HALF), BF16),
            jax.ShapeDtypeStruct((ALL_ROWS, HALF), BF16),
        ],
        compiler_params=params(),
        cost_estimate=pl.CostEstimate(flops=6_000_000_000, bytes_accessed=36_000_000, transcendentals=221184),
    )(core, own, other, wgu, wd)


def backward(gathered, row_of, weight, gate, up, wgu, wd):
    return pl.pallas_call(
        backward_kernel,
        grid=(STEPS,),
        in_specs=[
            pl.BlockSpec((STEP_GROUPS * TOK, D), lambda i: (i, 0)), ROW_SPEC, ROW_SPEC, UNIT_SPEC, UNIT_SPEC,
            whole(wgu.shape), whole(wd.shape),
        ],
        out_specs=[
            WIDE_SPEC, pl.BlockSpec((2, ROWS, UNITS), lambda i: (0, i, 0)), SHARE_SPEC,
        ],
        out_shape=[
            jax.ShapeDtypeStruct((ALL_ROWS, D), BF16),
            jax.ShapeDtypeStruct((2, ALL_ROWS, UNITS), BF16),
            jax.ShapeDtypeStruct((TENSOR, ALL_ROWS, SHARE), BF16),
        ],
        compiler_params=params(),
        cost_estimate=pl.CostEstimate(flops=8_000_000_000, bytes_accessed=42_000_000, transcendentals=221184),
    )(gathered, row_of, weight, gate, up, wgu, wd)


def combine(returned, own_weight):
    return pl.pallas_call(
        combine_kernel,
        out_shape=jax.ShapeDtypeStruct((TOK, SHARE), BF16),
        compiler_params=pltpu.CompilerParams(vmem_limit_bytes=VMEM_LIMIT),
        cost_estimate=pl.CostEstimate(flops=200_000_000, bytes_accessed=1_400_000, transcendentals=0),
    )(returned, own_weight)


def depth_parts(level, returned, own_weight):
    return pl.pallas_call(
        depth_kernel,
        grid_spec=pltpu.PrefetchScalarGridSpec(
            num_scalar_prefetch=1,
            grid=(DEPTH,),
            in_specs=[
                pl.BlockSpec((EXPERTS, CAP, SHARE), lambda d, z: (0, 0, (z[0] + d) % DEPTH)),
                pl.BlockSpec((TOK, EXPERTS), lambda d, z: (0, 0)),
            ],
            out_specs=pl.BlockSpec((None, TOK, SHARE), lambda d, z: (d, 0, 0)),
        ),
        out_shape=jax.ShapeDtypeStruct((DEPTH, TOK, SHARE), BF16),
        compiler_params=params(),
        cost_estimate=pl.CostEstimate(flops=800_000_000, bytes_accessed=5_300_000, transcendentals=0),
    )(level, returned, own_weight)


def over_experts(x):
    return lax.all_to_all(x, "expert", split_axis=0, concat_axis=0, tiled=True)


def swap_cores(x):
    return lax.ppermute(x, "tensor", [(t, t ^ 1) for t in range(TENSOR)])


def up_levels(x, d):
    return lax.ppermute(x, "tensor", [(t, (t + 2 * d) % TENSOR) for t in range(TENSOR)])


def on_device(tokens, expert_ids, gate_probs, grad_out, gate_up, down_proj):
    part = TOK // TENSOR
    member = lax.axis_index("tensor")
    core, level = member % 2, member // 2
    core_list, level_list = core.reshape(1).astype(jnp.int32), level.reshape(1).astype(jnp.int32)
    wgu, wd = gate_up[0], down_proj[0]

    mine = lax.dynamic_slice_in_dim(grad_out, member * part, part, 0)
    grad_rows = lax.all_gather(mine, ("expert", "tensor"), axis=0, tiled=True)

    named = expert_ids[:, :, None] == jnp.arange(EXPERTS, dtype=jnp.int32)
    own_weight = jnp.sum(jnp.where(named, gate_probs[:, :, None], 0.0), axis=1)
    weight_rows = own_weight.T
    x_half = lax.dynamic_slice_in_dim(tokens, core * HALF, HALF, 1)
    own_rows = over_experts(pick(x_half, weight_rows)).reshape(ALL_ROWS, HALF)
    other_rows = swap_cores(own_rows)
    weight_rows, own_rows = lax.optimization_barrier((weight_rows, own_rows))
    weight = over_experts(weight_rows)
    mask = weight > 0.0
    place = jnp.arange(TOK, dtype=jnp.int32)
    earlier = (place[:, None] < place[None, :]).astype(BF16)
    slot = jnp.dot(mask.astype(BF16), earlier, preferred_element_type=F32).astype(jnp.int32)
    offset = CAP * (jnp.arange(GROUPS, dtype=jnp.int32) % 2)
    row_of = jnp.where(mask, slot + offset[:, None], -1).reshape(GROUPS // 2, 1, 2 * TOK)
    weight = weight.reshape(GROUPS // 2, 1, 2 * TOK)

    inputs, gate, up, hidden, keep, send = forward(core_list, own_rows, other_rows, wgu, wd)
    pair_sum = (keep.astype(F32) + swap_cores(send).astype(F32)).astype(BF16)
    pair_sum, gate = lax.optimization_barrier((pair_sum, gate))
    out_back = over_experts(pair_sum.reshape(GROUPS, CAP, HALF))

    cot, dgu, partial_back = backward(grad_rows, row_of, weight, gate, up, wgu, wd)
    back_sum = lax.psum_scatter(partial_back, "tensor", scatter_dimension=0, tiled=False)
    grad_back = over_experts(back_sum.reshape(GROUPS, CAP, SHARE))
    grad_down = jnp.einsum("rf,rd->fd", hidden, cot, preferred_element_type=F32).astype(BF16)
    grad_gate_up = jnp.einsum("crf,rd->cfd", dgu, inputs, preferred_element_type=F32).astype(BF16)

    parts = depth_parts(level_list, out_back, own_weight)
    mixed = parts[0].astype(F32)
    for d in range(1, DEPTH):
        mixed += up_levels(parts[d], d).astype(F32)
    grad_tokens = combine(grad_back, own_weight)
    return (mixed.astype(BF16), grad_tokens, grad_gate_up[None], grad_down[None])


def solution(mesh):
    return jax.shard_map(
        on_device,
        mesh=mesh,
        in_specs=(
            P("expert", None),
            P("expert", None),
            P("expert", None),
            P("expert", None),
            P("expert", None, "tensor", None),
            P("expert", "tensor", None),
        ),
        out_specs=(
            P("expert", "tensor"),
            P("expert", "tensor"),
            P("expert", None, "tensor", None),
            P("expert", "tensor", None),
        ),
        check_vma=False,
    )
```

```python
import jax
import jax.numpy as jnp
from jax import lax
from jax.experimental import pallas as pl
from jax.experimental.pallas import tpu as pltpu
from jax.sharding import PartitionSpec as P

EXPERTS = 16
CAP = 72
GROUPS = 16
TOK = 128
D = 4096
UNITS = 192
TENSOR = 8
SHARE = D // TENSOR
HALF = D // 2
DEPTH = TENSOR // 2
STEP_GROUPS = 4
PAIRS = STEP_GROUPS // 2
ROWS = STEP_GROUPS * CAP
STEPS = GROUPS // STEP_GROUPS
ALL_ROWS = GROUPS * CAP
F32 = jnp.float32
BF16 = jnp.bfloat16
VMEM_LIMIT = 56 * 1024 * 1024


def nt(a, b):
    return lax.dot_general(a, b, (((1,), (1,)), ((), ())), preferred_element_type=F32)


def nn(a, b):
    return lax.dot_general(a, b, (((1,), (0,)), ((), ())), preferred_element_type=F32)


def pick_kernel(x_ref, w_ref, o_ref):
    mask = w_ref[...] > 0.0
    earlier = lax.broadcasted_iota(jnp.int32, (TOK, TOK), 0) < lax.broadcasted_iota(jnp.int32, (TOK, TOK), 1)
    ones = jnp.where(mask, 1.0, 0.0).astype(BF16)
    slot = nn(ones, jnp.where(earlier, 1.0, 0.0).astype(BF16))
    slot = jnp.where(mask, slot, -1.0).astype(jnp.int32)
    x = x_ref[...]
    for e in range(EXPERTS):
        hit = lax.broadcasted_iota(jnp.int32, (CAP, TOK), 0) == slot[e : e + 1]
        o_ref[e] = nn(jnp.where(hit, 1.0, 0.0).astype(BF16), x).astype(BF16)


def forward_kernel(
    core_ref, own_ref, other_ref, wgu_ref, wd_ref, in_ref, gate_ref, up_ref, hid_ref, keep_ref, send_ref
):
    core = core_ref[0]
    in_ref[:, pl.ds(pl.multiple_of(core * HALF, HALF), HALF)] = own_ref[...]
    in_ref[:, pl.ds(pl.multiple_of((1 - core) * HALF, HALF), HALF)] = other_ref[...]
    rows = in_ref[...]
    gate = nt(rows, wgu_ref[0])
    up = nt(rows, wgu_ref[1])
    gate_ref[...] = gate
    up_ref[...] = up
    hidden = (gate * jax.nn.sigmoid(gate) * up).astype(BF16)
    hid_ref[...] = hidden
    for ref, parity in ((send_ref, 1 - core), (keep_ref, core)):
        for z in range(DEPTH):
            cols = pl.ds(pl.multiple_of((2 * z + parity) * SHARE, SHARE), SHARE)
            ref[:, SHARE * z : SHARE * (z + 1)] = nn(hidden, wd_ref[:, cols]).astype(BF16)


def backward_kernel(g_ref, row_ref, w_ref, gate_ref, up_ref, wgu_ref, wd_ref, cot_ref, dgu_ref, back_ref):
    for j in range(PAIRS):
        g = g_ref[2 * TOK * j : 2 * TOK * (j + 1), :]
        hit = lax.broadcasted_iota(jnp.int32, (2 * CAP, 2 * TOK), 0) == row_ref[j]
        onehot = jnp.where(hit, 1.0, 0.0).astype(BF16)
        weight = jnp.sum(jnp.where(hit, w_ref[j], 0.0), axis=1, keepdims=True)
        cot_ref[2 * CAP * j : 2 * CAP * (j + 1), :] = (nn(onehot, g) * weight).astype(BF16)
    dhid = nt(cot_ref[...], wd_ref[...])
    gate = gate_ref[...]
    up = up_ref[...]
    sig = jax.nn.sigmoid(gate)
    dgate = (dhid * up * sig * (1.0 + gate * (1.0 - sig))).astype(BF16)
    dup = (dhid * gate * sig).astype(BF16)
    dgu_ref[0] = dgate
    dgu_ref[1] = dup
    for c in range(TENSOR):
        cols = slice(SHARE * c, SHARE * (c + 1))
        back_ref[c] = (nn(dgate, wgu_ref[0, :, cols]) + nn(dup, wgu_ref[1, :, cols])).astype(BF16)


def own_places(w_ref):
    w = w_ref[...]
    mask = w > 0.0
    ones = jnp.where(mask, 1.0, 0.0)
    lower = lax.broadcasted_iota(jnp.int32, (TOK, TOK), 1) < lax.broadcasted_iota(jnp.int32, (TOK, TOK), 0)
    slot = nn(jnp.where(lower, 1.0, 0.0).astype(BF16), ones.astype(BF16))
    return w, ones, jnp.where(mask, slot, -1.0).astype(jnp.int32)


def combine_kernel(r_ref, w_ref, o_ref):
    _, ones, slot = own_places(w_ref)
    total = jnp.zeros(o_ref.shape, F32)
    for e in range(EXPERTS):
        hit = lax.broadcasted_iota(jnp.int32, (TOK, CAP), 1) == slot[:, e : e + 1]
        onehot = jnp.where(hit, 1.0, 0.0).astype(BF16)
        total += nn(onehot, r_ref[e]) * ones[:, e : e + 1]
    o_ref[...] = total.astype(BF16)


def depth_kernel(z_ref, r_ref, w_ref, o_ref):
    w, _, slot = own_places(w_ref)
    total = jnp.zeros((TOK, SHARE), F32)
    for e in range(EXPERTS):
        hit = lax.broadcasted_iota(jnp.int32, (TOK, CAP), 1) == slot[:, e : e + 1]
        onehot = jnp.where(hit, 1.0, 0.0).astype(BF16)
        total += nn(onehot, r_ref[e]) * w[:, e : e + 1]
    o_ref[...] = total.astype(BF16)


def params():
    return pltpu.CompilerParams(vmem_limit_bytes=VMEM_LIMIT, dimension_semantics=("arbitrary",))


def whole(shape):
    return pl.BlockSpec(shape, lambda i: (0,) * len(shape), pipeline_mode=pl.Buffered(1))


ROW_SPEC = pl.BlockSpec((PAIRS, 1, 2 * TOK), lambda i: (i, 0, 0))
WIDE_SPEC = pl.BlockSpec((ROWS, D), lambda i: (i, 0))
UNIT_SPEC = pl.BlockSpec((ROWS, UNITS), lambda i: (i, 0))
SHARE_SPEC = pl.BlockSpec((TENSOR, ROWS, SHARE), lambda i: (0, i, 0))


def pick(x_half, weight_rows):
    return pl.pallas_call(
        pick_kernel,
        out_shape=jax.ShapeDtypeStruct((EXPERTS, CAP, HALF), BF16),
        compiler_params=pltpu.CompilerParams(vmem_limit_bytes=VMEM_LIMIT),
        cost_estimate=pl.CostEstimate(flops=600_000_000, bytes_accessed=5_300_000, transcendentals=0),
    )(x_half, weight_rows)


def forward(core, own, other, wgu, wd):
    wide = pl.BlockSpec((ROWS, D), lambda i, _: (i, 0))
    half = pl.BlockSpec((ROWS, HALF), lambda i, _: (i, 0))
    units = pl.BlockSpec((ROWS, UNITS), lambda i, _: (i, 0))
    once = pl.Buffered(1)
    return pl.pallas_call(
        forward_kernel,
        grid_spec=pltpu.PrefetchScalarGridSpec(
            num_scalar_prefetch=1,
            grid=(STEPS,),
            in_specs=[
                half,
                half,
                pl.BlockSpec(wgu.shape, lambda i, _: (0, 0, 0), pipeline_mode=once),
                pl.BlockSpec(wd.shape, lambda i, _: (0, 0), pipeline_mode=once),
            ],
            out_specs=[wide, units, units, units, half, half],
        ),
        out_shape=[
            jax.ShapeDtypeStruct((ALL_ROWS, D), BF16),
            jax.ShapeDtypeStruct((ALL_ROWS, UNITS), F32),
            jax.ShapeDtypeStruct((ALL_ROWS, UNITS), F32),
            jax.ShapeDtypeStruct((ALL_ROWS, UNITS), BF16),
            jax.ShapeDtypeStruct((ALL_ROWS, HALF), BF16),
            jax.ShapeDtypeStruct((ALL_ROWS, HALF), BF16),
        ],
        compiler_params=params(),
        cost_estimate=pl.CostEstimate(flops=6_000_000_000, bytes_accessed=36_000_000, transcendentals=221184),
    )(core, own, other, wgu, wd)


def backward(gathered, row_of, weight, gate, up, wgu, wd):
    return pl.pallas_call(
        backward_kernel,
        grid=(STEPS,),
        in_specs=[
            pl.BlockSpec((STEP_GROUPS * TOK, D), lambda i: (i, 0)), ROW_SPEC, ROW_SPEC, UNIT_SPEC, UNIT_SPEC,
            whole(wgu.shape), whole(wd.shape),
        ],
        out_specs=[
            WIDE_SPEC, pl.BlockSpec((2, ROWS, UNITS), lambda i: (0, i, 0)), SHARE_SPEC,
        ],
        out_shape=[
            jax.ShapeDtypeStruct((ALL_ROWS, D), BF16),
            jax.ShapeDtypeStruct((2, ALL_ROWS, UNITS), BF16),
            jax.ShapeDtypeStruct((TENSOR, ALL_ROWS, SHARE), BF16),
        ],
        compiler_params=params(),
        cost_estimate=pl.CostEstimate(flops=8_000_000_000, bytes_accessed=42_000_000, transcendentals=221184),
    )(gathered, row_of, weight, gate, up, wgu, wd)


def combine(returned, own_weight):
    return pl.pallas_call(
        combine_kernel,
        out_shape=jax.ShapeDtypeStruct((TOK, SHARE), BF16),
        compiler_params=pltpu.CompilerParams(vmem_limit_bytes=VMEM_LIMIT),
        cost_estimate=pl.CostEstimate(flops=200_000_000, bytes_accessed=1_400_000, transcendentals=0),
    )(returned, own_weight)


def depth_parts(level, returned, own_weight):
    return pl.pallas_call(
        depth_kernel,
        grid_spec=pltpu.PrefetchScalarGridSpec(
            num_scalar_prefetch=1,
            grid=(DEPTH,),
            in_specs=[
                pl.BlockSpec((EXPERTS, CAP, SHARE), lambda d, z: (0, 0, (z[0] + d) % DEPTH)),
                pl.BlockSpec((TOK, EXPERTS), lambda d, z: (0, 0)),
            ],
            out_specs=pl.BlockSpec((None, TOK, SHARE), lambda d, z: (d, 0, 0)),
        ),
        out_shape=jax.ShapeDtypeStruct((DEPTH, TOK, SHARE), BF16),
        compiler_params=params(),
        cost_estimate=pl.CostEstimate(flops=170_000_000_000, bytes_accessed=5_300_000, transcendentals=0),
    )(level, returned, own_weight)


def over_experts(x):
    return lax.all_to_all(x, "expert", split_axis=0, concat_axis=0, tiled=True)


def swap_cores(x):
    return lax.ppermute(x, "tensor", [(t, t ^ 1) for t in range(TENSOR)])


def up_levels(x, d):
    return lax.ppermute(x, "tensor", [(t, (t + 2 * d) % TENSOR) for t in range(TENSOR)])


def on_device(tokens, expert_ids, gate_probs, grad_out, gate_up, down_proj):
    part = TOK // TENSOR
    member = lax.axis_index("tensor")
    core, level = member % 2, member // 2
    core_list, level_list = core.reshape(1).astype(jnp.int32), level.reshape(1).astype(jnp.int32)
    wgu, wd = gate_up[0], down_proj[0]

    mine = lax.dynamic_slice_in_dim(grad_out, member * part, part, 0)
    grad_rows = lax.all_gather(mine, ("expert", "tensor"), axis=0, tiled=True)

    named = expert_ids[:, :, None] == jnp.arange(EXPERTS, dtype=jnp.int32)
    own_weight = jnp.sum(jnp.where(named, gate_probs[:, :, None], 0.0), axis=1)
    weight_rows = own_weight.T
    x_half = lax.dynamic_slice_in_dim(tokens, core * HALF, HALF, 1)
    own_rows = over_experts(pick(x_half, weight_rows)).reshape(ALL_ROWS, HALF)
    other_rows = swap_cores(own_rows)
    weight_rows, own_rows = lax.optimization_barrier((weight_rows, own_rows))
    weight = over_experts(weight_rows)
    mask = weight > 0.0
    place = jnp.arange(TOK, dtype=jnp.int32)
    earlier = (place[:, None] < place[None, :]).astype(BF16)
    slot = jnp.dot(mask.astype(BF16), earlier, preferred_element_type=F32).astype(jnp.int32)
    offset = CAP * (jnp.arange(GROUPS, dtype=jnp.int32) % 2)
    row_of = jnp.where(mask, slot + offset[:, None], -1).reshape(GROUPS // 2, 1, 2 * TOK)
    weight = weight.reshape(GROUPS // 2, 1, 2 * TOK)

    inputs, gate, up, hidden, keep, send = forward(core_list, own_rows, other_rows, wgu, wd)
    pair_sum = (keep.astype(F32) + swap_cores(send).astype(F32)).astype(BF16)
    pair_sum, gate = lax.optimization_barrier((pair_sum, gate))
    out_back = over_experts(pair_sum.reshape(GROUPS, CAP, HALF))

    cot, dgu, partial_back = backward(grad_rows, row_of, weight, gate, up, wgu, wd)
    back_sum = lax.psum_scatter(partial_back, "tensor", scatter_dimension=0, tiled=False)
    grad_back = over_experts(back_sum.reshape(GROUPS, CAP, SHARE))
    grad_down = jnp.einsum("rf,rd->fd", hidden, cot, preferred_element_type=F32).astype(BF16)
    grad_gate_up = jnp.einsum("crf,rd->cfd", dgu, inputs, preferred_element_type=F32).astype(BF16)

    out_back, _ = lax.optimization_barrier((out_back, back_sum))
    parts = depth_parts(level_list, out_back, own_weight)
    mixed = parts[0].astype(F32)
    for d in range(1, DEPTH):
        mixed += up_levels(parts[d], d).astype(F32)
    grad_tokens = combine(grad_back, own_weight)
    return (mixed.astype(BF16), grad_tokens, grad_gate_up[None], grad_down[None])


def solution(mesh):
    return jax.shard_map(
        on_device,
        mesh=mesh,
        in_specs=(
            P("expert", None),
            P("expert", None),
            P("expert", None),
            P("expert", None),
            P("expert", None, "tensor", None),
            P("expert", "tensor", None),
        ),
        out_specs=(
            P("expert", "tensor"),
            P("expert", "tensor"),
            P("expert", None, "tensor", None),
            P("expert", "tensor", None),
        ),
        check_vma=False,
    )
```

```python
import jax
import jax.numpy as jnp
from jax import lax
from jax.experimental import pallas as pl
from jax.experimental.pallas import tpu as pltpu
from jax.sharding import PartitionSpec as P

EXPERTS = 16
CAP = 72
GROUPS = 16
TOK = 128
D = 4096
UNITS = 192
WIDE = 256
TENSOR = 8
SHARE = D // TENSOR
HALF = D // 2
DEPTH = TENSOR // 2
STEP_GROUPS = 4
PAIRS = STEP_GROUPS // 2
ROWS = STEP_GROUPS * CAP
STEPS = GROUPS // STEP_GROUPS
ALL_ROWS = GROUPS * CAP
F32 = jnp.float32
BF16 = jnp.bfloat16
VMEM_LIMIT = 56 * 1024 * 1024


def nt(a, b):
    return lax.dot_general(a, b, (((1,), (1,)), ((), ())), preferred_element_type=F32)


def tn(a, b):
    return lax.dot_general(a, b, (((0,), (0,)), ((), ())), preferred_element_type=F32)


def nn(a, b):
    return lax.dot_general(a, b, (((1,), (0,)), ((), ())), preferred_element_type=F32)


def pick_kernel(x_ref, w_ref, o_ref):
    mask = w_ref[...] > 0.0
    earlier = lax.broadcasted_iota(jnp.int32, (TOK, TOK), 0) < lax.broadcasted_iota(jnp.int32, (TOK, TOK), 1)
    ones = jnp.where(mask, 1.0, 0.0).astype(BF16)
    slot = nn(ones, jnp.where(earlier, 1.0, 0.0).astype(BF16))
    slot = jnp.where(mask, slot, -1.0).astype(jnp.int32)
    x = x_ref[...]
    for e in range(EXPERTS):
        hit = lax.broadcasted_iota(jnp.int32, (CAP, TOK), 0) == slot[e : e + 1]
        o_ref[e] = nn(jnp.where(hit, 1.0, 0.0).astype(BF16), x).astype(BF16)


def lend_kernel(core_ref, after_ref, wgu_ref, wd_ref, o_ref):
    o_ref[0:2] = wgu_ref[...]
    o_ref[2] = wd_ref[...]


def hidden_kernel(core_ref, own_ref, other_ref, wgu_ref, in_ref, gate_ref, up_ref, hid_ref):
    core = core_ref[0]
    in_ref[:, pl.ds(pl.multiple_of(core * HALF, HALF), HALF)] = own_ref[...]
    in_ref[:, pl.ds(pl.multiple_of((1 - core) * HALF, HALF), HALF)] = other_ref[...]
    rows = in_ref[...]
    gate = nt(rows, wgu_ref[0])
    up = nt(rows, wgu_ref[1])
    gate_ref[...] = gate
    up_ref[...] = up
    hid_ref[:, :UNITS] = (gate * jax.nn.sigmoid(gate) * up).astype(BF16)
    hid_ref[:, UNITS:] = jnp.zeros((ROWS, WIDE - UNITS), BF16)


def out_kernel(core_ref, own_ref, other_ref, wd_ref, lent_ref, o_ref):
    own, other = own_ref[:, :UNITS], other_ref[:, :UNITS]
    for z in range(DEPTH):
        cols = pl.ds(pl.multiple_of((2 * z + core_ref[0]) * SHARE, SHARE), SHARE)
        share = slice(SHARE * z, SHARE * (z + 1))
        o_ref[:, share] = (nn(own, wd_ref[:, cols]) + nn(other, lent_ref[:, share])).astype(BF16)


def unit_grad_kernel(g_ref, row_ref, w_ref, gate_ref, up_ref, wd_ref, cot_ref, dgu_ref):
    for j in range(PAIRS):
        g = g_ref[2 * TOK * j : 2 * TOK * (j + 1), :]
        hit = lax.broadcasted_iota(jnp.int32, (2 * CAP, 2 * TOK), 0) == row_ref[j]
        onehot = jnp.where(hit, 1.0, 0.0).astype(BF16)
        weight = jnp.sum(jnp.where(hit, w_ref[j], 0.0), axis=1, keepdims=True)
        cot_ref[2 * CAP * j : 2 * CAP * (j + 1), :] = (nn(onehot, g) * weight).astype(BF16)
    dhid = nt(cot_ref[...], wd_ref[...])
    gate = gate_ref[...]
    up = up_ref[...]
    sig = jax.nn.sigmoid(gate)
    dgu_ref[:, :, UNITS:] = jnp.zeros((2, ROWS, WIDE - UNITS), BF16)
    dgu_ref[0, :, :UNITS] = (dhid * up * sig * (1.0 + gate * (1.0 - sig))).astype(BF16)
    dgu_ref[1, :, :UNITS] = (dhid * gate * sig).astype(BF16)


def weight_grad_kernel(in_ref, cot_ref, dgu_ref, hid_ref, gu_ref, down_ref):
    x = in_ref[...]
    gu_ref[0] = tn(dgu_ref[0, :, :UNITS], x).astype(BF16)
    gu_ref[1] = tn(dgu_ref[1, :, :UNITS], x).astype(BF16)
    down_ref[...] = tn(hid_ref[:, :UNITS], cot_ref[...]).astype(BF16)


def back_kernel(core_ref, own_ref, other_ref, wgu_ref, lent_ref, o_ref):
    for z in range(DEPTH):
        cols = pl.ds(pl.multiple_of((2 * z + core_ref[0]) * SHARE, SHARE), SHARE)
        share = slice(SHARE * z, SHARE * (z + 1))
        total = nn(own_ref[0, :, :UNITS], wgu_ref[0, :, cols]) + nn(own_ref[1, :, :UNITS], wgu_ref[1, :, cols])
        total += nn(other_ref[0, :, :UNITS], lent_ref[0, :, share])
        total += nn(other_ref[1, :, :UNITS], lent_ref[1, :, share])
        o_ref[z] = total.astype(BF16)


def own_places(w_ref):
    w = w_ref[...]
    mask = w > 0.0
    ones = jnp.where(mask, 1.0, 0.0)
    lower = lax.broadcasted_iota(jnp.int32, (TOK, TOK), 1) < lax.broadcasted_iota(jnp.int32, (TOK, TOK), 0)
    slot = nn(jnp.where(lower, 1.0, 0.0).astype(BF16), ones.astype(BF16))
    return w, ones, jnp.where(mask, slot, -1.0).astype(jnp.int32)


def combine_kernel(r_ref, w_ref, o_ref):
    _, ones, slot = own_places(w_ref)
    total = jnp.zeros(o_ref.shape, F32)
    for e in range(EXPERTS):
        hit = lax.broadcasted_iota(jnp.int32, (TOK, CAP), 1) == slot[:, e : e + 1]
        onehot = jnp.where(hit, 1.0, 0.0).astype(BF16)
        total += nn(onehot, r_ref[e]) * ones[:, e : e + 1]
    o_ref[...] = total.astype(BF16)


def depth_kernel(z_ref, r_ref, w_ref, o_ref):
    w, _, slot = own_places(w_ref)
    total = jnp.zeros((TOK, SHARE), F32)
    for e in range(EXPERTS):
        hit = lax.broadcasted_iota(jnp.int32, (TOK, CAP), 1) == slot[:, e : e + 1]
        onehot = jnp.where(hit, 1.0, 0.0).astype(BF16)
        total += nn(onehot, r_ref[e]) * w[:, e : e + 1]
    o_ref[...] = total.astype(BF16)


def params():
    return pltpu.CompilerParams(vmem_limit_bytes=VMEM_LIMIT, dimension_semantics=("arbitrary",))


def whole(shape):
    return pl.BlockSpec(shape, lambda *_: (0,) * len(shape), pipeline_mode=pl.Buffered(1))


def by_rows(*shape):
    return pl.BlockSpec(shape, lambda i, *_: (0,) * (len(shape) - 2) + (i, 0))


def shaped(*shape, dtype=BF16):
    return jax.ShapeDtypeStruct(shape, dtype)


def stepped(kernel, scalars, steps, in_specs, out_specs, out_shape, flops, moved):
    return pl.pallas_call(
        kernel,
        grid_spec=pltpu.PrefetchScalarGridSpec(
            num_scalar_prefetch=scalars, grid=(steps,), in_specs=in_specs, out_specs=out_specs
        ),
        out_shape=out_shape,
        compiler_params=params(),
        cost_estimate=pl.CostEstimate(flops=flops, bytes_accessed=moved, transcendentals=0),
    )


ROW_SPEC = pl.BlockSpec((PAIRS, 1, 2 * TOK), lambda i, *_: (i, 0, 0))


def pick(x_half, weight_rows):
    return pl.pallas_call(
        pick_kernel,
        out_shape=jax.ShapeDtypeStruct((EXPERTS, CAP, HALF), BF16),
        compiler_params=pltpu.CompilerParams(vmem_limit_bytes=VMEM_LIMIT),
        cost_estimate=pl.CostEstimate(flops=600_000_000, bytes_accessed=5_300_000, transcendentals=0),
    )(x_half, weight_rows)


def lend(other_core, after, wgu, wd):
    return stepped(
        lend_kernel, 1, DEPTH,
        [
            pl.BlockSpec(memory_space=pl.ANY),
            pl.BlockSpec((2, UNITS, SHARE), lambda z, c: (0, 0, 2 * z + c[0])),
            pl.BlockSpec((UNITS, SHARE), lambda z, c: (0, 2 * z + c[0])),
        ],
        pl.BlockSpec((3, UNITS, SHARE), lambda z, c: (0, 0, z)),
        shaped(3, UNITS, HALF), 0, 4_700_000,
    )(other_core, after, wgu, wd)


def hidden_units(core, own, other, wgu):
    return stepped(
        hidden_kernel, 1, STEPS,
        [by_rows(ROWS, HALF), by_rows(ROWS, HALF), whole(wgu.shape)],
        [by_rows(ROWS, D), by_rows(ROWS, UNITS), by_rows(ROWS, UNITS), by_rows(ROWS, WIDE)],
        [
            shaped(ALL_ROWS, D), shaped(ALL_ROWS, UNITS, dtype=F32), shaped(ALL_ROWS, UNITS, dtype=F32),
            shaped(ALL_ROWS, WIDE),
        ],
        4_000_000_000, 25_000_000,
    )(core, own, other, wgu)


def out_rows(core, own, other, wd, lent):
    return stepped(
        out_kernel, 1, STEPS,
        [
            by_rows(ROWS, WIDE), by_rows(ROWS, WIDE), whole(wd.shape),
            pl.BlockSpec((None, UNITS, HALF), lambda *_: (2, 0, 0), pipeline_mode=pl.Buffered(1)),
        ],
        by_rows(ROWS, HALF), shaped(ALL_ROWS, HALF), 2_000_000_000, 8_000_000,
    )(core, own, other, wd, lent)


def unit_grads(grad_rows, row_of, weight, gate, up, wd):
    return stepped(
        unit_grad_kernel, 0, STEPS,
        [
            by_rows(STEP_GROUPS * TOK, D), ROW_SPEC, ROW_SPEC, by_rows(ROWS, UNITS), by_rows(ROWS, UNITS),
            whole(wd.shape),
        ],
        [by_rows(ROWS, D), by_rows(2, ROWS, WIDE)],
        [shaped(ALL_ROWS, D), shaped(2, ALL_ROWS, WIDE)],
        4_000_000_000, 30_000_000,
    )(grad_rows, row_of, weight, gate, up, wd)


def back_rows(core, own, other, wgu, lent):
    return stepped(
        back_kernel, 1, STEPS,
        [by_rows(2, ROWS, WIDE), by_rows(2, ROWS, WIDE), whole(wgu.shape), whole((2, UNITS, HALF))],
        by_rows(DEPTH, ROWS, SHARE), shaped(DEPTH, ALL_ROWS, SHARE), 4_000_000_000, 10_000_000,
    )(core, own, other, wgu, lent)


def weight_grads(inputs, cot, dgu, hidden):
    cols = pl.BlockSpec((ALL_ROWS, SHARE), lambda i: (0, i))
    return stepped(
        weight_grad_kernel, 0, TENSOR,
        [cols, cols, whole(dgu.shape), whole(hidden.shape)],
        [
            pl.BlockSpec((2, UNITS, SHARE), lambda i: (0, 0, i)),
            pl.BlockSpec((UNITS, SHARE), lambda i: (0, i)),
        ],
        [shaped(2, UNITS, D), shaped(UNITS, D)], 6_000_000_000, 25_000_000,
    )(inputs, cot, dgu, hidden)


def combine(returned, own_weight):
    return pl.pallas_call(
        combine_kernel,
        out_shape=jax.ShapeDtypeStruct((TOK, SHARE), BF16),
        compiler_params=pltpu.CompilerParams(vmem_limit_bytes=VMEM_LIMIT),
        cost_estimate=pl.CostEstimate(flops=200_000_000, bytes_accessed=1_400_000, transcendentals=0),
    )(returned, own_weight)


def depth_parts(level, returned, own_weight):
    return pl.pallas_call(
        depth_kernel,
        grid_spec=pltpu.PrefetchScalarGridSpec(
            num_scalar_prefetch=1,
            grid=(DEPTH,),
            in_specs=[
                pl.BlockSpec((EXPERTS, CAP, SHARE), lambda d, z: (0, 0, (z[0] + d) % DEPTH)),
                pl.BlockSpec((TOK, EXPERTS), lambda d, z: (0, 0)),
            ],
            out_specs=pl.BlockSpec((None, TOK, SHARE), lambda d, z: (d, 0, 0)),
        ),
        out_shape=jax.ShapeDtypeStruct((DEPTH, TOK, SHARE), BF16),
        compiler_params=params(),
        cost_estimate=pl.CostEstimate(flops=130000000000, bytes_accessed=5_300_000, transcendentals=0),
    )(level, returned, own_weight)


def over_experts(x):
    return lax.all_to_all(x, "expert", split_axis=0, concat_axis=0, tiled=True)


def swap_cores(x):
    return lax.ppermute(x, "tensor", [(t, t ^ 1) for t in range(TENSOR)])


def up_levels(x, d):
    return lax.ppermute(x, "tensor", [(t, (t + 2 * d) % TENSOR) for t in range(TENSOR)])


def on_device(tokens, expert_ids, gate_probs, grad_out, gate_up, down_proj):
    part = TOK // TENSOR
    member = lax.axis_index("tensor")
    core, level = member % 2, member // 2
    core_list, level_list = core.reshape(1).astype(jnp.int32), level.reshape(1).astype(jnp.int32)
    wgu, wd = gate_up[0], down_proj[0]

    mine = lax.dynamic_slice_in_dim(grad_out, member * part, part, 0)
    grad_rows = lax.all_gather(mine, ("expert", "tensor"), axis=0, tiled=True)

    named = expert_ids[:, :, None] == jnp.arange(EXPERTS, dtype=jnp.int32)
    own_weight = jnp.sum(jnp.where(named, gate_probs[:, :, None], 0.0), axis=1)
    weight_rows = own_weight.T
    x_half = lax.dynamic_slice_in_dim(tokens, core * HALF, HALF, 1)
    picked = pick(x_half, weight_rows)
    own_rows = over_experts(picked).reshape(ALL_ROWS, HALF)
    lent = swap_cores(lend(1 - core_list, picked, wgu, wd))
    own_rows, lent = lax.optimization_barrier((own_rows, lent))
    other_rows = swap_cores(own_rows)
    weight_rows, own_rows = lax.optimization_barrier((weight_rows, own_rows))
    weight = over_experts(weight_rows)
    mask = weight > 0.0
    place = jnp.arange(TOK, dtype=jnp.int32)
    earlier = (place[:, None] < place[None, :]).astype(BF16)
    slot = jnp.dot(mask.astype(BF16), earlier, preferred_element_type=F32).astype(jnp.int32)
    offset = CAP * (jnp.arange(GROUPS, dtype=jnp.int32) % 2)
    row_of = jnp.where(mask, slot + offset[:, None], -1).reshape(GROUPS // 2, 1, 2 * TOK)
    weight = weight.reshape(GROUPS // 2, 1, 2 * TOK)

    inputs, gate, up, hidden = hidden_units(core_list, own_rows, other_rows, wgu)
    pair_out = out_rows(core_list, hidden, swap_cores(hidden), wd, lent)
    pair_out, gate = lax.optimization_barrier((pair_out, gate))
    out_back = over_experts(pair_out.reshape(GROUPS, CAP, HALF))

    cot, dgu = unit_grads(grad_rows, row_of, weight, gate, up, wd)
    pair_back = back_rows(core_list, dgu, swap_cores(dgu), wgu, lent)
    back_sum = lax.psum_scatter(
        pair_back, "tensor", scatter_dimension=0, tiled=False,
        axis_index_groups=[[2 * z + c for z in range(DEPTH)] for c in range(2)],
    )
    grad_back = over_experts(back_sum.reshape(GROUPS, CAP, SHARE))
    grad_gate_up, grad_down = weight_grads(inputs, cot, dgu, hidden)
    parts = depth_parts(level_list, out_back, own_weight)
    mixed = parts[0].astype(F32)
    for d in range(1, DEPTH):
        mixed += up_levels(parts[d], d).astype(F32)
    grad_tokens = combine(grad_back, own_weight)
    return (mixed.astype(BF16), grad_tokens, grad_gate_up[None], grad_down[None])


def solution(mesh):
    return jax.shard_map(
        on_device,
        mesh=mesh,
        in_specs=(
            P("expert", None),
            P("expert", None),
            P("expert", None),
            P("expert", None),
            P("expert", None, "tensor", None),
            P("expert", "tensor", None),
        ),
        out_specs=(
            P("expert", "tensor"),
            P("expert", "tensor"),
            P("expert", None, "tensor", None),
            P("expert", "tensor", None),
        ),
        check_vma=False,
    )
```

```python
import jax
import jax.numpy as jnp
from jax import lax
from jax.experimental import pallas as pl
from jax.experimental.pallas import tpu as pltpu
from jax.sharding import PartitionSpec as P

EXPERTS = 16
CAP = 72
GROUPS = 16
TOK = 128
D = 4096
UNITS = 192
WIDE = 256
TENSOR = 8
SHARE = D // TENSOR
HALF = D // 2
DEPTH = TENSOR // 2
STEP_GROUPS = 4
PAIRS = STEP_GROUPS // 2
ROWS = STEP_GROUPS * CAP
STEPS = GROUPS // STEP_GROUPS
ALL_ROWS = GROUPS * CAP
F32 = jnp.float32
BF16 = jnp.bfloat16
VMEM_LIMIT = 56 * 1024 * 1024


def nt(a, b):
    return lax.dot_general(a, b, (((1,), (1,)), ((), ())), preferred_element_type=F32)


def tn(a, b):
    return lax.dot_general(a, b, (((0,), (0,)), ((), ())), preferred_element_type=F32)


def nn(a, b):
    return lax.dot_general(a, b, (((1,), (0,)), ((), ())), preferred_element_type=F32)


def pick_kernel(x_ref, w_ref, o_ref):
    mask = w_ref[...] > 0.0
    earlier = lax.broadcasted_iota(jnp.int32, (TOK, TOK), 0) < lax.broadcasted_iota(jnp.int32, (TOK, TOK), 1)
    ones = jnp.where(mask, 1.0, 0.0).astype(BF16)
    slot = nn(ones, jnp.where(earlier, 1.0, 0.0).astype(BF16))
    slot = jnp.where(mask, slot, -1.0).astype(jnp.int32)
    x = x_ref[...]
    for e in range(EXPERTS):
        hit = lax.broadcasted_iota(jnp.int32, (CAP, TOK), 0) == slot[e : e + 1]
        o_ref[e] = nn(jnp.where(hit, 1.0, 0.0).astype(BF16), x).astype(BF16)


def lend_kernel(core_ref, after_ref, wgu_ref, wd_ref, o_ref):
    o_ref[0:2] = wgu_ref[...]
    o_ref[2] = wd_ref[...]


def hidden_kernel(core_ref, own_ref, other_ref, wgu_ref, in_ref, gate_ref, up_ref, hid_ref):
    core = core_ref[0]
    in_ref[:, pl.ds(pl.multiple_of(core * HALF, HALF), HALF)] = own_ref[...]
    in_ref[:, pl.ds(pl.multiple_of((1 - core) * HALF, HALF), HALF)] = other_ref[...]
    rows = in_ref[...]
    gate = nt(rows, wgu_ref[0])
    up = nt(rows, wgu_ref[1])
    gate_ref[...] = gate
    up_ref[...] = up
    hid_ref[:, :UNITS] = (gate * jax.nn.sigmoid(gate) * up).astype(BF16)
    hid_ref[:, UNITS:] = jnp.zeros((ROWS, WIDE - UNITS), BF16)


def out_kernel(core_ref, own_ref, other_ref, wd_ref, lent_ref, o_ref):
    own, other = own_ref[:, :UNITS], other_ref[:, :UNITS]
    for z in range(DEPTH):
        cols = pl.ds(pl.multiple_of((2 * z + core_ref[0]) * SHARE, SHARE), SHARE)
        share = slice(SHARE * z, SHARE * (z + 1))
        o_ref[:, share] = (nn(own, wd_ref[:, cols]) + nn(other, lent_ref[:, share])).astype(BF16)


def unit_grad_kernel(g_ref, row_ref, w_ref, gate_ref, up_ref, wd_ref, cot_ref, dgu_ref):
    for j in range(PAIRS):
        g = g_ref[2 * TOK * j : 2 * TOK * (j + 1), :]
        hit = lax.broadcasted_iota(jnp.int32, (2 * CAP, 2 * TOK), 0) == row_ref[j]
        onehot = jnp.where(hit, 1.0, 0.0).astype(BF16)
        weight = jnp.sum(jnp.where(hit, w_ref[j], 0.0), axis=1, keepdims=True)
        cot_ref[2 * CAP * j : 2 * CAP * (j + 1), :] = (nn(onehot, g) * weight).astype(BF16)
    dhid = nt(cot_ref[...], wd_ref[...])
    gate = gate_ref[...]
    up = up_ref[...]
    sig = jax.nn.sigmoid(gate)
    dgu_ref[:, :, UNITS:] = jnp.zeros((2, ROWS, WIDE - UNITS), BF16)
    dgu_ref[0, :, :UNITS] = (dhid * up * sig * (1.0 + gate * (1.0 - sig))).astype(BF16)
    dgu_ref[1, :, :UNITS] = (dhid * gate * sig).astype(BF16)


def weight_grad_kernel(in_ref, cot_ref, dgu_ref, hid_ref, gu_ref, down_ref):
    x = in_ref[...]
    gu_ref[0] = tn(dgu_ref[0, :, :UNITS], x).astype(BF16)
    gu_ref[1] = tn(dgu_ref[1, :, :UNITS], x).astype(BF16)
    down_ref[...] = tn(hid_ref[:, :UNITS], cot_ref[...]).astype(BF16)


def back_kernel(core_ref, own_ref, other_ref, wgu_ref, lent_ref, o_ref):
    for z in range(DEPTH):
        cols = pl.ds(pl.multiple_of((2 * z + core_ref[0]) * SHARE, SHARE), SHARE)
        share = slice(SHARE * z, SHARE * (z + 1))
        total = nn(own_ref[0, :, :UNITS], wgu_ref[0, :, cols]) + nn(own_ref[1, :, :UNITS], wgu_ref[1, :, cols])
        total += nn(other_ref[0, :, :UNITS], lent_ref[0, :, share])
        total += nn(other_ref[1, :, :UNITS], lent_ref[1, :, share])
        o_ref[z] = total.astype(BF16)


def own_places(w_ref):
    w = w_ref[...]
    mask = w > 0.0
    ones = jnp.where(mask, 1.0, 0.0)
    lower = lax.broadcasted_iota(jnp.int32, (TOK, TOK), 1) < lax.broadcasted_iota(jnp.int32, (TOK, TOK), 0)
    slot = nn(jnp.where(lower, 1.0, 0.0).astype(BF16), ones.astype(BF16))
    return w, ones, jnp.where(mask, slot, -1.0).astype(jnp.int32)


def combine_kernel(r_ref, w_ref, o_ref):
    _, ones, slot = own_places(w_ref)
    total = jnp.zeros(o_ref.shape, F32)
    for e in range(EXPERTS):
        hit = lax.broadcasted_iota(jnp.int32, (TOK, CAP), 1) == slot[:, e : e + 1]
        onehot = jnp.where(hit, 1.0, 0.0).astype(BF16)
        total += nn(onehot, r_ref[e]) * ones[:, e : e + 1]
    o_ref[...] = total.astype(BF16)


def depth_kernel(z_ref, r_ref, w_ref, after_ref, o_ref):
    w, _, slot = own_places(w_ref)
    total = jnp.zeros((TOK, SHARE), F32)
    for e in range(EXPERTS):
        hit = lax.broadcasted_iota(jnp.int32, (TOK, CAP), 1) == slot[:, e : e + 1]
        onehot = jnp.where(hit, 1.0, 0.0).astype(BF16)
        total += nn(onehot, r_ref[e]) * w[:, e : e + 1]
    o_ref[...] = total.astype(BF16)


def params():
    return pltpu.CompilerParams(vmem_limit_bytes=VMEM_LIMIT, dimension_semantics=("arbitrary",))


def whole(shape):
    return pl.BlockSpec(shape, lambda *_: (0,) * len(shape), pipeline_mode=pl.Buffered(1))


def by_rows(*shape):
    return pl.BlockSpec(shape, lambda i, *_: (0,) * (len(shape) - 2) + (i, 0))


def shaped(*shape, dtype=BF16):
    return jax.ShapeDtypeStruct(shape, dtype)


def stepped(kernel, scalars, steps, in_specs, out_specs, out_shape, flops, moved):
    return pl.pallas_call(
        kernel,
        grid_spec=pltpu.PrefetchScalarGridSpec(
            num_scalar_prefetch=scalars, grid=(steps,), in_specs=in_specs, out_specs=out_specs
        ),
        out_shape=out_shape,
        compiler_params=params(),
        cost_estimate=pl.CostEstimate(flops=flops, bytes_accessed=moved, transcendentals=0),
    )


ROW_SPEC = pl.BlockSpec((PAIRS, 1, 2 * TOK), lambda i, *_: (i, 0, 0))


def pick(x_half, weight_rows):
    return pl.pallas_call(
        pick_kernel,
        out_shape=jax.ShapeDtypeStruct((EXPERTS, CAP, HALF), BF16),
        compiler_params=pltpu.CompilerParams(vmem_limit_bytes=VMEM_LIMIT),
        cost_estimate=pl.CostEstimate(flops=600_000_000, bytes_accessed=5_300_000, transcendentals=0),
    )(x_half, weight_rows)


def lend(other_core, after, wgu, wd):
    return stepped(
        lend_kernel, 1, DEPTH,
        [
            pl.BlockSpec(memory_space=pl.ANY),
            pl.BlockSpec((2, UNITS, SHARE), lambda z, c: (0, 0, 2 * z + c[0])),
            pl.BlockSpec((UNITS, SHARE), lambda z, c: (0, 2 * z + c[0])),
        ],
        pl.BlockSpec((3, UNITS, SHARE), lambda z, c: (0, 0, z)),
        shaped(3, UNITS, HALF), 0, 4_700_000,
    )(other_core, after, wgu, wd)


def hidden_units(core, own, other, wgu):
    return stepped(
        hidden_kernel, 1, STEPS,
        [by_rows(ROWS, HALF), by_rows(ROWS, HALF), whole(wgu.shape)],
        [by_rows(ROWS, D), by_rows(ROWS, UNITS), by_rows(ROWS, UNITS), by_rows(ROWS, WIDE)],
        [
            shaped(ALL_ROWS, D), shaped(ALL_ROWS, UNITS, dtype=F32), shaped(ALL_ROWS, UNITS, dtype=F32),
            shaped(ALL_ROWS, WIDE),
        ],
        4_000_000_000, 25_000_000,
    )(core, own, other, wgu)


def out_rows(core, own, other, wd, lent):
    return stepped(
        out_kernel, 1, STEPS,
        [
            by_rows(ROWS, WIDE), by_rows(ROWS, WIDE), whole(wd.shape),
            pl.BlockSpec((None, UNITS, HALF), lambda *_: (2, 0, 0), pipeline_mode=pl.Buffered(1)),
        ],
        by_rows(ROWS, HALF), shaped(ALL_ROWS, HALF), 2_000_000_000, 8_000_000,
    )(core, own, other, wd, lent)


def unit_grads(grad_rows, row_of, weight, gate, up, wd):
    return stepped(
        unit_grad_kernel, 0, STEPS,
        [
            by_rows(STEP_GROUPS * TOK, D), ROW_SPEC, ROW_SPEC, by_rows(ROWS, UNITS), by_rows(ROWS, UNITS),
            whole(wd.shape),
        ],
        [by_rows(ROWS, D), by_rows(2, ROWS, WIDE)],
        [shaped(ALL_ROWS, D), shaped(2, ALL_ROWS, WIDE)],
        4_000_000_000, 30_000_000,
    )(grad_rows, row_of, weight, gate, up, wd)


def back_rows(core, own, other, wgu, lent):
    return stepped(
        back_kernel, 1, STEPS,
        [by_rows(2, ROWS, WIDE), by_rows(2, ROWS, WIDE), whole(wgu.shape), whole((2, UNITS, HALF))],
        by_rows(DEPTH, ROWS, SHARE), shaped(DEPTH, ALL_ROWS, SHARE), 4_000_000_000, 10_000_000,
    )(core, own, other, wgu, lent)


def weight_grads(inputs, cot, dgu, hidden):
    cols = pl.BlockSpec((ALL_ROWS, SHARE), lambda i: (0, i))
    return stepped(
        weight_grad_kernel, 0, TENSOR,
        [cols, cols, whole(dgu.shape), whole(hidden.shape)],
        [
            pl.BlockSpec((2, UNITS, SHARE), lambda i: (0, 0, i)),
            pl.BlockSpec((UNITS, SHARE), lambda i: (0, i)),
        ],
        [shaped(2, UNITS, D), shaped(UNITS, D)], 6_000_000_000, 25_000_000,
    )(inputs, cot, dgu, hidden)


def combine(returned, own_weight):
    return pl.pallas_call(
        combine_kernel,
        in_specs=[pl.BlockSpec(memory_space=pltpu.VMEM)] * 2,
        out_shape=jax.ShapeDtypeStruct((TOK, SHARE), BF16),
        compiler_params=pltpu.CompilerParams(vmem_limit_bytes=VMEM_LIMIT),
        cost_estimate=pl.CostEstimate(flops=200_000_000, bytes_accessed=1_400_000, transcendentals=0),
    )(returned, own_weight)


def depth_parts(level, returned, own_weight, after):
    return pl.pallas_call(
        depth_kernel,
        grid_spec=pltpu.PrefetchScalarGridSpec(
            num_scalar_prefetch=1,
            grid=(DEPTH,),
            in_specs=[
                pl.BlockSpec((EXPERTS, CAP, SHARE), lambda d, z: (0, 0, (z[0] + d) % DEPTH)),
                pl.BlockSpec((TOK, EXPERTS), lambda d, z: (0, 0)),
                pl.BlockSpec(memory_space=pl.ANY),
            ],
            out_specs=pl.BlockSpec((None, TOK, SHARE), lambda d, z: (d, 0, 0)),
        ),
        out_shape=jax.ShapeDtypeStruct((DEPTH, TOK, SHARE), BF16),
        compiler_params=params(),
        cost_estimate=pl.CostEstimate(flops=90_000_000_000, bytes_accessed=5_300_000, transcendentals=0),
    )(level, returned, own_weight, after)


def over_experts(x):
    return lax.all_to_all(x, "expert", split_axis=0, concat_axis=0, tiled=True)


def swap_cores(x):
    return lax.ppermute(x, "tensor", [(t, t ^ 1) for t in range(TENSOR)])


def up_levels(x, d):
    return lax.ppermute(x, "tensor", [(t, (t + 2 * d) % TENSOR) for t in range(TENSOR)])


def on_device(tokens, expert_ids, gate_probs, grad_out, gate_up, down_proj):
    part = TOK // TENSOR
    member = lax.axis_index("tensor")
    core, level = member % 2, member // 2
    core_list, level_list = core.reshape(1).astype(jnp.int32), level.reshape(1).astype(jnp.int32)
    wgu, wd = gate_up[0], down_proj[0]

    mine = lax.dynamic_slice_in_dim(grad_out, member * part, part, 0)
    grad_rows = lax.all_gather(mine, ("expert", "tensor"), axis=0, tiled=True)

    named = expert_ids[:, :, None] == jnp.arange(EXPERTS, dtype=jnp.int32)
    own_weight = jnp.sum(jnp.where(named, gate_probs[:, :, None], 0.0), axis=1)
    weight_rows = own_weight.T
    x_half = lax.dynamic_slice_in_dim(tokens, core * HALF, HALF, 1)
    picked = pick(x_half, weight_rows)
    own_rows = over_experts(picked).reshape(ALL_ROWS, HALF)
    lent = swap_cores(lend(1 - core_list, picked, wgu, wd))
    other_rows = swap_cores(own_rows)
    weight_rows, own_rows = lax.optimization_barrier((weight_rows, own_rows))
    weight = over_experts(weight_rows)
    mask = weight > 0.0
    place = jnp.arange(TOK, dtype=jnp.int32)
    earlier = (place[:, None] < place[None, :]).astype(BF16)
    slot = jnp.dot(mask.astype(BF16), earlier, preferred_element_type=F32).astype(jnp.int32)
    offset = CAP * (jnp.arange(GROUPS, dtype=jnp.int32) % 2)
    row_of = jnp.where(mask, slot + offset[:, None], -1).reshape(GROUPS // 2, 1, 2 * TOK)
    weight = weight.reshape(GROUPS // 2, 1, 2 * TOK)

    inputs, gate, up, hidden = hidden_units(core_list, own_rows, other_rows, wgu)
    pair_out = out_rows(core_list, hidden, swap_cores(hidden), wd, lent)
    pair_out, gate = lax.optimization_barrier((pair_out, gate))
    out_back = over_experts(pair_out.reshape(GROUPS, CAP, HALF))

    cot, dgu = unit_grads(grad_rows, row_of, weight, gate, up, wd)
    pair_back = back_rows(core_list, dgu, swap_cores(dgu), wgu, lent)
    back_sum = lax.psum_scatter(
        pair_back, "tensor", scatter_dimension=0, tiled=False,
        axis_index_groups=[[2 * z + c for z in range(DEPTH)] for c in range(2)],
    )
    grad_gate_up, grad_down = weight_grads(inputs, cot, dgu, hidden)
    parts = depth_parts(level_list, out_back, own_weight, grad_down)
    parts, back_sum = lax.optimization_barrier((parts, back_sum))
    grad_back = over_experts(back_sum.reshape(GROUPS, CAP, SHARE))
    mixed = parts[0].astype(F32)
    for d in range(1, DEPTH):
        mixed += up_levels(parts[d], d).astype(F32)
    grad_tokens = combine(grad_back, own_weight)
    return (mixed.astype(BF16), grad_tokens, grad_gate_up[None], grad_down[None])


def solution(mesh):
    return jax.shard_map(
        on_device,
        mesh=mesh,
        in_specs=(
            P("expert", None),
            P("expert", None),
            P("expert", None),
            P("expert", None),
            P("expert", None, "tensor", None),
            P("expert", "tensor", None),
        ),
        out_specs=(
            P("expert", "tensor"),
            P("expert", "tensor"),
            P("expert", None, "tensor", None),
            P("expert", "tensor", None),
        ),
        check_vma=False,
    )
```

```python
import jax
import jax.numpy as jnp
from jax import lax
from jax.experimental import pallas as pl
from jax.experimental.pallas import tpu as pltpu
from jax.sharding import PartitionSpec as P

EXPERTS = 16
CAP = 72
GROUPS = 16
TOK = 128
D = 4096
UNITS = 192
WIDE = 256
TENSOR = 8
SHARE = D // TENSOR
HALF = D // 2
PART = SHARE // 2
DEPTH = TENSOR // 2
STEP_GROUPS = 4
PAIRS = STEP_GROUPS // 2
ROWS = STEP_GROUPS * CAP
STEPS = GROUPS // STEP_GROUPS
ALL_ROWS = GROUPS * CAP
F32 = jnp.float32
BF16 = jnp.bfloat16
VMEM_LIMIT = 56 * 1024 * 1024


def nt(a, b):
    return lax.dot_general(a, b, (((1,), (1,)), ((), ())), preferred_element_type=F32)


def tn(a, b):
    return lax.dot_general(a, b, (((0,), (0,)), ((), ())), preferred_element_type=F32)


def nn(a, b):
    return lax.dot_general(a, b, (((1,), (0,)), ((), ())), preferred_element_type=F32)


def pick_kernel(x_ref, w_ref, o_ref):
    mask = w_ref[...] > 0.0
    earlier = lax.broadcasted_iota(jnp.int32, (TOK, TOK), 0) < lax.broadcasted_iota(jnp.int32, (TOK, TOK), 1)
    ones = jnp.where(mask, 1.0, 0.0).astype(BF16)
    slot = nn(ones, jnp.where(earlier, 1.0, 0.0).astype(BF16))
    slot = jnp.where(mask, slot, -1.0).astype(jnp.int32)
    x = x_ref[...]
    for e in range(EXPERTS):
        hit = lax.broadcasted_iota(jnp.int32, (CAP, TOK), 0) == slot[e : e + 1]
        o_ref[e] = nn(jnp.where(hit, 1.0, 0.0).astype(BF16), x).astype(BF16)


def lend_kernel(core_ref, after_ref, wgu_ref, wd_ref, o_ref):
    o_ref[0:2] = wgu_ref[...]
    o_ref[2] = wd_ref[...]


def hidden_kernel(core_ref, own_ref, other_ref, wgu_ref, in_ref, gate_ref, up_ref, hid_ref):
    core = core_ref[0]
    in_ref[:, pl.ds(pl.multiple_of(core * HALF, HALF), HALF)] = own_ref[...]
    in_ref[:, pl.ds(pl.multiple_of((1 - core) * HALF, HALF), HALF)] = other_ref[...]
    rows = in_ref[...]
    gate = nt(rows, wgu_ref[0])
    up = nt(rows, wgu_ref[1])
    gate_ref[...] = gate
    up_ref[...] = up
    hid_ref[:, :UNITS] = (gate * jax.nn.sigmoid(gate) * up).astype(BF16)
    hid_ref[:, UNITS:] = jnp.zeros((ROWS, WIDE - UNITS), BF16)


def out_kernel(core_ref, own_ref, other_ref, wd_ref, lent_ref, direct_ref, part_ref):
    own, other = own_ref[:, :UNITS], other_ref[:, :UNITS]
    for z in range(DEPTH):
        cols = pl.ds(pl.multiple_of((2 * z + core_ref[0]) * SHARE, SHARE), SHARE)
        share = slice(SHARE * z, SHARE * (z + 1))
        total = (nn(own, wd_ref[:, cols]) + nn(other, lent_ref[:, share])).astype(BF16)
        direct_ref[:, PART * z : PART * (z + 1)] = total[:, :PART]
        part_ref[z] = total[:, PART:]


def unit_grad_kernel(g_ref, row_ref, w_ref, gate_ref, up_ref, wd_ref, cot_ref, dgu_ref):
    for j in range(PAIRS):
        g = g_ref[2 * TOK * j : 2 * TOK * (j + 1), :]
        hit = lax.broadcasted_iota(jnp.int32, (2 * CAP, 2 * TOK), 0) == row_ref[j]
        onehot = jnp.where(hit, 1.0, 0.0).astype(BF16)
        weight = jnp.sum(jnp.where(hit, w_ref[j], 0.0), axis=1, keepdims=True)
        cot_ref[2 * CAP * j : 2 * CAP * (j + 1), :] = (nn(onehot, g) * weight).astype(BF16)
    dhid = nt(cot_ref[...], wd_ref[...])
    gate = gate_ref[...]
    up = up_ref[...]
    sig = jax.nn.sigmoid(gate)
    dgu_ref[:, :, UNITS:] = jnp.zeros((2, ROWS, WIDE - UNITS), BF16)
    dgu_ref[0, :, :UNITS] = (dhid * up * sig * (1.0 + gate * (1.0 - sig))).astype(BF16)
    dgu_ref[1, :, :UNITS] = (dhid * gate * sig).astype(BF16)


def weight_grad_kernel(in_ref, cot_ref, dgu_ref, hid_ref, gu_ref, down_ref):
    x = in_ref[...]
    gu_ref[0] = tn(dgu_ref[0, :, :UNITS], x).astype(BF16)
    gu_ref[1] = tn(dgu_ref[1, :, :UNITS], x).astype(BF16)
    down_ref[...] = tn(hid_ref[:, :UNITS], cot_ref[...]).astype(BF16)


def back_kernel(core_ref, after_ref, own_ref, other_ref, wgu_ref, lent_ref, direct_ref, part_ref):
    for z in range(DEPTH):
        cols = pl.ds(pl.multiple_of((2 * z + core_ref[0]) * SHARE, SHARE), SHARE)
        share = slice(SHARE * z, SHARE * (z + 1))
        total = nn(own_ref[0, :, :UNITS], wgu_ref[0, :, cols]) + nn(own_ref[1, :, :UNITS], wgu_ref[1, :, cols])
        total += nn(other_ref[0, :, :UNITS], lent_ref[0, :, share])
        total += nn(other_ref[1, :, :UNITS], lent_ref[1, :, share])
        total = total.astype(BF16)
        direct_ref[:, PART * z : PART * (z + 1)] = total[:, :PART]
        part_ref[z] = total[:, PART:]


def own_places(w_ref):
    w = w_ref[...]
    mask = w > 0.0
    ones = jnp.where(mask, 1.0, 0.0)
    lower = lax.broadcasted_iota(jnp.int32, (TOK, TOK), 1) < lax.broadcasted_iota(jnp.int32, (TOK, TOK), 0)
    slot = nn(jnp.where(lower, 1.0, 0.0).astype(BF16), ones.astype(BF16))
    return w, ones, jnp.where(mask, slot, -1.0).astype(jnp.int32)


def combine_kernel(weighted, r_ref, w_ref, o_ref):
    w, ones, slot = own_places(w_ref)
    scale = w if weighted else ones
    total = jnp.zeros(o_ref.shape, F32)
    for e in range(EXPERTS):
        hit = lax.broadcasted_iota(jnp.int32, (TOK, CAP), 1) == slot[:, e : e + 1]
        onehot = jnp.where(hit, 1.0, 0.0).astype(BF16)
        total += nn(onehot, r_ref[e]) * scale[:, e : e + 1]
    o_ref[...] = total.astype(BF16)


def params():
    return pltpu.CompilerParams(vmem_limit_bytes=VMEM_LIMIT, dimension_semantics=("arbitrary",))


def whole(shape):
    return pl.BlockSpec(shape, lambda *_: (0,) * len(shape), pipeline_mode=pl.Buffered(1))


def by_rows(*shape):
    return pl.BlockSpec(shape, lambda i, *_: (0,) * (len(shape) - 2) + (i, 0))


def shaped(*shape, dtype=BF16):
    return jax.ShapeDtypeStruct(shape, dtype)


def stepped(kernel, scalars, steps, in_specs, out_specs, out_shape, flops, moved):
    return pl.pallas_call(
        kernel,
        grid_spec=pltpu.PrefetchScalarGridSpec(
            num_scalar_prefetch=scalars, grid=(steps,), in_specs=in_specs, out_specs=out_specs
        ),
        out_shape=out_shape,
        compiler_params=params(),
        cost_estimate=pl.CostEstimate(flops=flops, bytes_accessed=moved, transcendentals=0),
    )


ROW_SPEC = pl.BlockSpec((PAIRS, 1, 2 * TOK), lambda i, *_: (i, 0, 0))


SPLIT = (
    [by_rows(ROWS, DEPTH * PART), by_rows(DEPTH, ROWS, PART)],
    [shaped(ALL_ROWS, DEPTH * PART), shaped(DEPTH, ALL_ROWS, PART)],
)


def pick(x_half, weight_rows):
    return pl.pallas_call(
        pick_kernel,
        out_shape=jax.ShapeDtypeStruct((EXPERTS, CAP, HALF), BF16),
        compiler_params=pltpu.CompilerParams(vmem_limit_bytes=VMEM_LIMIT),
        cost_estimate=pl.CostEstimate(flops=600_000_000, bytes_accessed=5_300_000, transcendentals=0),
    )(x_half, weight_rows)


def lend(other_core, after, wgu, wd):
    return stepped(
        lend_kernel, 1, DEPTH,
        [
            pl.BlockSpec(memory_space=pl.ANY),
            pl.BlockSpec((2, UNITS, SHARE), lambda z, c: (0, 0, 2 * z + c[0])),
            pl.BlockSpec((UNITS, SHARE), lambda z, c: (0, 2 * z + c[0])),
        ],
        pl.BlockSpec((3, UNITS, SHARE), lambda z, c: (0, 0, z)),
        shaped(3, UNITS, HALF), 0, 4_700_000,
    )(other_core, after, wgu, wd)


def hidden_units(core, own, other, wgu):
    return stepped(
        hidden_kernel, 1, STEPS,
        [by_rows(ROWS, HALF), by_rows(ROWS, HALF), whole(wgu.shape)],
        [by_rows(ROWS, D), by_rows(ROWS, UNITS), by_rows(ROWS, UNITS), by_rows(ROWS, WIDE)],
        [
            shaped(ALL_ROWS, D), shaped(ALL_ROWS, UNITS, dtype=F32), shaped(ALL_ROWS, UNITS, dtype=F32),
            shaped(ALL_ROWS, WIDE),
        ],
        4_000_000_000, 25_000_000,
    )(core, own, other, wgu)


def out_rows(core, own, other, wd, lent):
    return stepped(
        out_kernel, 1, STEPS,
        [
            by_rows(ROWS, WIDE), by_rows(ROWS, WIDE), whole(wd.shape),
            pl.BlockSpec((None, UNITS, HALF), lambda *_: (2, 0, 0), pipeline_mode=pl.Buffered(1)),
        ],
        *SPLIT, 2_000_000_000, 8_000_000,
    )(core, own, other, wd, lent)


def unit_grads(grad_rows, row_of, weight, gate, up, wd):
    return stepped(
        unit_grad_kernel, 0, STEPS,
        [
            by_rows(STEP_GROUPS * TOK, D), ROW_SPEC, ROW_SPEC, by_rows(ROWS, UNITS), by_rows(ROWS, UNITS),
            whole(wd.shape),
        ],
        [by_rows(ROWS, D), by_rows(2, ROWS, WIDE)],
        [shaped(ALL_ROWS, D), shaped(2, ALL_ROWS, WIDE)],
        4_000_000_000, 30_000_000,
    )(grad_rows, row_of, weight, gate, up, wd)


def back_rows(core, after, own, other, wgu, lent):
    return stepped(
        back_kernel, 1, STEPS,
        [
            pl.BlockSpec(memory_space=pl.ANY), by_rows(2, ROWS, WIDE), by_rows(2, ROWS, WIDE),
            whole(wgu.shape), whole((2, UNITS, HALF)),
        ],
        *SPLIT, 4_000_000_000, 10_000_000,
    )(core, after, own, other, wgu, lent)


def weight_grads(inputs, cot, dgu, hidden):
    cols = pl.BlockSpec((ALL_ROWS, SHARE), lambda i: (0, i))
    return stepped(
        weight_grad_kernel, 0, TENSOR,
        [cols, cols, whole(dgu.shape), whole(hidden.shape)],
        [
            pl.BlockSpec((2, UNITS, SHARE), lambda i: (0, 0, i)),
            pl.BlockSpec((UNITS, SHARE), lambda i: (0, i)),
        ],
        [shaped(2, UNITS, D), shaped(UNITS, D)], 6_000_000_000, 25_000_000,
    )(inputs, cot, dgu, hidden)


def combine(weighted, returned, own_weight):
    return pl.pallas_call(
        lambda *refs: combine_kernel(weighted, *refs),
        in_specs=[pl.BlockSpec(memory_space=pltpu.VMEM)] * 2,
        out_shape=shaped(TOK, PART),
        compiler_params=pltpu.CompilerParams(vmem_limit_bytes=VMEM_LIMIT),
        cost_estimate=pl.CostEstimate(flops=200_000_000, bytes_accessed=1_400_000, transcendentals=0),
    )(returned, own_weight)


def sum_levels(weighted, level, returned, own_weight):
    parts = pl.pallas_call(
        lambda z_ref, *refs: combine_kernel(weighted, *refs),
        grid_spec=pltpu.PrefetchScalarGridSpec(
            num_scalar_prefetch=1,
            grid=(DEPTH,),
            in_specs=[
                pl.BlockSpec((EXPERTS, CAP, PART), lambda d, z: (0, 0, (z[0] + d) % DEPTH)),
                pl.BlockSpec((TOK, EXPERTS), lambda d, z: (0, 0)),
            ],
            out_specs=pl.BlockSpec((None, TOK, PART), lambda d, z: (d, 0, 0)),
        ),
        out_shape=shaped(DEPTH, TOK, PART),
        compiler_params=params(),
        cost_estimate=pl.CostEstimate(flops=1_000_000_000, bytes_accessed=2_600_000, transcendentals=0),
    )(level, returned, own_weight)
    total = parts[0].astype(F32)
    for d in range(1, DEPTH):
        total += up_levels(parts[d], d).astype(F32)
    return total.astype(BF16)


def sum_over_depth(x):
    return lax.psum_scatter(
        x, "tensor", scatter_dimension=0, tiled=False,
        axis_index_groups=[[2 * z + c for z in range(DEPTH)] for c in range(2)],
    )


def over_experts(x):
    return lax.all_to_all(x, "expert", split_axis=0, concat_axis=0, tiled=True)


def return_rows(x):
    return over_experts(x.reshape(GROUPS, CAP, x.shape[-1]))


def swap_cores(x):
    return lax.ppermute(x, "tensor", [(t, t ^ 1) for t in range(TENSOR)])


def up_levels(x, d):
    return lax.ppermute(x, "tensor", [(t, (t + 2 * d) % TENSOR) for t in range(TENSOR)])


def on_device(tokens, expert_ids, gate_probs, grad_out, gate_up, down_proj):
    part = TOK // TENSOR
    member = lax.axis_index("tensor")
    core, level = member % 2, member // 2
    core_list, level_list = core.reshape(1).astype(jnp.int32), level.reshape(1).astype(jnp.int32)
    wgu, wd = gate_up[0], down_proj[0]

    mine = lax.dynamic_slice_in_dim(grad_out, member * part, part, 0)
    grad_rows = lax.all_gather(mine, ("expert", "tensor"), axis=0, tiled=True)

    named = expert_ids[:, :, None] == jnp.arange(EXPERTS, dtype=jnp.int32)
    own_weight = jnp.sum(jnp.where(named, gate_probs[:, :, None], 0.0), axis=1)
    weight_rows = own_weight.T
    x_half = lax.dynamic_slice_in_dim(tokens, core * HALF, HALF, 1)
    picked = pick(x_half, weight_rows)
    own_rows = over_experts(picked).reshape(ALL_ROWS, HALF)
    lent = swap_cores(lend(1 - core_list, picked, wgu, wd))
    other_rows = swap_cores(own_rows)
    weight_rows, own_rows = lax.optimization_barrier((weight_rows, own_rows))
    weight = over_experts(weight_rows)
    mask = weight > 0.0
    place = jnp.arange(TOK, dtype=jnp.int32)
    earlier = (place[:, None] < place[None, :]).astype(BF16)
    slot = jnp.dot(mask.astype(BF16), earlier, preferred_element_type=F32).astype(jnp.int32)
    offset = CAP * (jnp.arange(GROUPS, dtype=jnp.int32) % 2)
    row_of = jnp.where(mask, slot + offset[:, None], -1).reshape(GROUPS // 2, 1, 2 * TOK)
    weight = weight.reshape(GROUPS // 2, 1, 2 * TOK)

    inputs, gate, up, hidden = hidden_units(core_list, own_rows, other_rows, wgu)
    out_direct, out_part = out_rows(core_list, hidden, swap_cores(hidden), wd, lent)
    out_direct, gate = lax.optimization_barrier((out_direct, gate))
    out_sum = sum_over_depth(out_part)
    out_direct = return_rows(out_direct)

    cot, dgu = unit_grads(grad_rows, row_of, weight, gate, up, wd)
    back_direct, back_part = back_rows(core_list, out_direct, dgu, swap_cores(dgu), wgu, lent)
    back_sum = sum_over_depth(back_part)
    grad_gate_up, grad_down = weight_grads(inputs, cot, dgu, hidden)

    out_sum, out_direct = lax.optimization_barrier((out_sum, out_direct))
    out_sum = return_rows(out_sum)
    back_direct, out_sum = lax.optimization_barrier((back_direct, out_sum))
    back_direct = return_rows(back_direct)
    back_sum, back_direct = lax.optimization_barrier((back_sum, back_direct))
    back_sum = return_rows(back_sum)

    mixed = jnp.concatenate(
        [sum_levels(True, level_list, out_direct, own_weight), combine(True, out_sum, own_weight)], axis=1
    )
    grad_tokens = jnp.concatenate(
        [sum_levels(False, level_list, back_direct, own_weight), combine(False, back_sum, own_weight)], axis=1
    )
    return (mixed, grad_tokens, grad_gate_up[None], grad_down[None])


def solution(mesh):
    return jax.shard_map(
        on_device,
        mesh=mesh,
        in_specs=(
            P("expert", None),
            P("expert", None),
            P("expert", None),
            P("expert", None),
            P("expert", None, "tensor", None),
            P("expert", "tensor", None),
        ),
        out_specs=(
            P("expert", "tensor"),
            P("expert", "tensor"),
            P("expert", None, "tensor", None),
            P("expert", "tensor", None),
        ),
        check_vma=False,
    )
```

```python
import jax
import jax.numpy as jnp
from jax import lax
from jax.experimental import pallas as pl
from jax.experimental.pallas import tpu as pltpu
from jax.sharding import PartitionSpec as P

EXPERTS = 16
CAP = 72
GROUPS = 16
TOK = 128
D = 4096
UNITS = 192
WIDE = 256
TENSOR = 8
SHARE = D // TENSOR
HALF = D // 2
DEPTH = TENSOR // 2
STEP_GROUPS = 4
PAIRS = STEP_GROUPS // 2
ROWS = STEP_GROUPS * CAP
STEPS = GROUPS // STEP_GROUPS
ALL_ROWS = GROUPS * CAP
F32 = jnp.float32
BF16 = jnp.bfloat16
VMEM_LIMIT = 56 * 1024 * 1024


def nt(a, b):
    return lax.dot_general(a, b, (((1,), (1,)), ((), ())), preferred_element_type=F32)


def tn(a, b):
    return lax.dot_general(a, b, (((0,), (0,)), ((), ())), preferred_element_type=F32)


def nn(a, b):
    return lax.dot_general(a, b, (((1,), (0,)), ((), ())), preferred_element_type=F32)


def pick_kernel(x_ref, w_ref, o_ref):
    mask = w_ref[...] > 0.0
    earlier = lax.broadcasted_iota(jnp.int32, (TOK, TOK), 0) < lax.broadcasted_iota(jnp.int32, (TOK, TOK), 1)
    ones = jnp.where(mask, 1.0, 0.0).astype(BF16)
    slot = nn(ones, jnp.where(earlier, 1.0, 0.0).astype(BF16))
    slot = jnp.where(mask, slot, -1.0).astype(jnp.int32)
    x = x_ref[...]
    for e in range(EXPERTS):
        hit = lax.broadcasted_iota(jnp.int32, (CAP, TOK), 0) == slot[e : e + 1]
        o_ref[e] = nn(jnp.where(hit, 1.0, 0.0).astype(BF16), x).astype(BF16)


def lend_kernel(core_ref, after_ref, wgu_ref, wd_ref, o_ref):
    o_ref[0:2] = wgu_ref[...]
    o_ref[2] = wd_ref[...]


def hidden_kernel(core_ref, own_ref, other_ref, wgu_ref, gate_ref, up_ref, hid_ref):
    mine = pl.ds(pl.multiple_of(core_ref[0] * HALF, HALF), HALF)
    theirs = pl.ds(pl.multiple_of((1 - core_ref[0]) * HALF, HALF), HALF)
    own, other = own_ref[...], other_ref[...]
    gate = nt(own, wgu_ref[0, :, mine]) + nt(other, wgu_ref[0, :, theirs])
    up = nt(own, wgu_ref[1, :, mine]) + nt(other, wgu_ref[1, :, theirs])
    gate_ref[...] = gate
    up_ref[...] = up
    hid_ref[:, :UNITS] = (gate * jax.nn.sigmoid(gate) * up).astype(BF16)
    hid_ref[:, UNITS:] = jnp.zeros((ROWS, WIDE - UNITS), BF16)


def out_kernel(core_ref, own_ref, other_ref, wd_ref, lent_ref, o_ref):
    own, other = own_ref[:, :UNITS], other_ref[:, :UNITS]
    for z in range(DEPTH):
        cols = pl.ds(pl.multiple_of((2 * z + core_ref[0]) * SHARE, SHARE), SHARE)
        share = slice(SHARE * z, SHARE * (z + 1))
        o_ref[:, share] = (nn(own, wd_ref[:, cols]) + nn(other, lent_ref[:, share])).astype(BF16)


def unit_grad_kernel(g_ref, row_ref, w_ref, gate_ref, up_ref, wd_ref, cot_ref, dgu_ref):
    for j in range(PAIRS):
        g = g_ref[2 * TOK * j : 2 * TOK * (j + 1), :]
        hit = lax.broadcasted_iota(jnp.int32, (2 * CAP, 2 * TOK), 0) == row_ref[j]
        onehot = jnp.where(hit, 1.0, 0.0).astype(BF16)
        weight = jnp.sum(jnp.where(hit, w_ref[j], 0.0), axis=1, keepdims=True)
        cot_ref[2 * CAP * j : 2 * CAP * (j + 1), :] = (nn(onehot, g) * weight).astype(BF16)
    dhid = nt(cot_ref[...], wd_ref[...])
    gate = gate_ref[...]
    up = up_ref[...]
    sig = jax.nn.sigmoid(gate)
    dgu_ref[:, :, UNITS:] = jnp.zeros((2, ROWS, WIDE - UNITS), BF16)
    dgu_ref[0, :, :UNITS] = (dhid * up * sig * (1.0 + gate * (1.0 - sig))).astype(BF16)
    dgu_ref[1, :, :UNITS] = (dhid * gate * sig).astype(BF16)


def weight_grad_kernel(core_ref, own_ref, other_ref, cot_ref, dgu_ref, hid_ref, gu_ref, down_ref):
    down_ref[...] = tn(hid_ref[:, :UNITS], cot_ref[...]).astype(BF16)
    owned = pl.program_id(0) // DEPTH == core_ref[0]

    def write(x):
        gu_ref[0] = tn(dgu_ref[0, :, :UNITS], x).astype(BF16)
        gu_ref[1] = tn(dgu_ref[1, :, :UNITS], x).astype(BF16)

    @pl.when(owned)
    def _():
        write(own_ref[...])

    @pl.when(jnp.logical_not(owned))
    def _():
        write(other_ref[...])


def back_kernel(core_ref, own_ref, other_ref, wgu_ref, lent_ref, o_ref):
    for z in range(DEPTH):
        cols = pl.ds(pl.multiple_of((2 * z + core_ref[0]) * SHARE, SHARE), SHARE)
        share = slice(SHARE * z, SHARE * (z + 1))
        total = nn(own_ref[0, :, :UNITS], wgu_ref[0, :, cols]) + nn(own_ref[1, :, :UNITS], wgu_ref[1, :, cols])
        total += nn(other_ref[0, :, :UNITS], lent_ref[0, :, share])
        total += nn(other_ref[1, :, :UNITS], lent_ref[1, :, share])
        o_ref[z] = total.astype(BF16)


def own_places(w_ref):
    w = w_ref[...]
    mask = w > 0.0
    ones = jnp.where(mask, 1.0, 0.0)
    lower = lax.broadcasted_iota(jnp.int32, (TOK, TOK), 1) < lax.broadcasted_iota(jnp.int32, (TOK, TOK), 0)
    slot = nn(jnp.where(lower, 1.0, 0.0).astype(BF16), ones.astype(BF16))
    return w, ones, jnp.where(mask, slot, -1.0).astype(jnp.int32)


def combine_kernel(r_ref, w_ref, o_ref):
    _, ones, slot = own_places(w_ref)
    total = jnp.zeros(o_ref.shape, F32)
    for e in range(EXPERTS):
        hit = lax.broadcasted_iota(jnp.int32, (TOK, CAP), 1) == slot[:, e : e + 1]
        onehot = jnp.where(hit, 1.0, 0.0).astype(BF16)
        total += nn(onehot, r_ref[e]) * ones[:, e : e + 1]
    o_ref[...] = total.astype(BF16)


def depth_kernel(z_ref, r_ref, w_ref, after_ref, o_ref):
    w, _, slot = own_places(w_ref)
    total = jnp.zeros((TOK, SHARE), F32)
    for e in range(EXPERTS):
        hit = lax.broadcasted_iota(jnp.int32, (TOK, CAP), 1) == slot[:, e : e + 1]
        onehot = jnp.where(hit, 1.0, 0.0).astype(BF16)
        total += nn(onehot, r_ref[e]) * w[:, e : e + 1]
    o_ref[...] = total.astype(BF16)


def params():
    return pltpu.CompilerParams(vmem_limit_bytes=VMEM_LIMIT, dimension_semantics=("arbitrary",))


def whole(shape):
    return pl.BlockSpec(shape, lambda *_: (0,) * len(shape), pipeline_mode=pl.Buffered(1))


def by_rows(*shape):
    return pl.BlockSpec(shape, lambda i, *_: (0,) * (len(shape) - 2) + (i, 0))


def shaped(*shape, dtype=BF16):
    return jax.ShapeDtypeStruct(shape, dtype)


def stepped(kernel, scalars, steps, in_specs, out_specs, out_shape, flops, moved):
    return pl.pallas_call(
        kernel,
        grid_spec=pltpu.PrefetchScalarGridSpec(
            num_scalar_prefetch=scalars, grid=(steps,), in_specs=in_specs, out_specs=out_specs
        ),
        out_shape=out_shape,
        compiler_params=params(),
        cost_estimate=pl.CostEstimate(flops=flops, bytes_accessed=moved, transcendentals=0),
    )


ROW_SPEC = pl.BlockSpec((PAIRS, 1, 2 * TOK), lambda i, *_: (i, 0, 0))


def pick(x_half, weight_rows):
    return pl.pallas_call(
        pick_kernel,
        out_shape=jax.ShapeDtypeStruct((EXPERTS, CAP, HALF), BF16),
        compiler_params=pltpu.CompilerParams(vmem_limit_bytes=VMEM_LIMIT),
        cost_estimate=pl.CostEstimate(flops=600_000_000, bytes_accessed=5_300_000, transcendentals=0),
    )(x_half, weight_rows)


def lend(other_core, after, wgu, wd):
    return stepped(
        lend_kernel, 1, DEPTH,
        [
            pl.BlockSpec(memory_space=pl.ANY),
            pl.BlockSpec((2, UNITS, SHARE), lambda z, c: (0, 0, 2 * z + c[0])),
            pl.BlockSpec((UNITS, SHARE), lambda z, c: (0, 2 * z + c[0])),
        ],
        pl.BlockSpec((3, UNITS, SHARE), lambda z, c: (0, 0, z)),
        shaped(3, UNITS, HALF), 0, 4_700_000,
    )(other_core, after, wgu, wd)


def hidden_units(core, own, other, wgu):
    return stepped(
        hidden_kernel, 1, STEPS,
        [by_rows(ROWS, HALF), by_rows(ROWS, HALF), whole(wgu.shape)],
        [by_rows(ROWS, UNITS), by_rows(ROWS, UNITS), by_rows(ROWS, WIDE)],
        [
            shaped(ALL_ROWS, UNITS, dtype=F32), shaped(ALL_ROWS, UNITS, dtype=F32),
            shaped(ALL_ROWS, WIDE),
        ],
        4_000_000_000, 15_000_000,
    )(core, own, other, wgu)


def out_rows(core, own, other, wd, lent):
    return stepped(
        out_kernel, 1, STEPS,
        [
            by_rows(ROWS, WIDE), by_rows(ROWS, WIDE), whole(wd.shape),
            pl.BlockSpec((None, UNITS, HALF), lambda *_: (2, 0, 0), pipeline_mode=pl.Buffered(1)),
        ],
        by_rows(ROWS, HALF), shaped(ALL_ROWS, HALF), 2_000_000_000, 8_000_000,
    )(core, own, other, wd, lent)


def unit_grads(grad_rows, row_of, weight, gate, up, wd):
    return stepped(
        unit_grad_kernel, 0, STEPS,
        [
            by_rows(STEP_GROUPS * TOK, D), ROW_SPEC, ROW_SPEC, by_rows(ROWS, UNITS), by_rows(ROWS, UNITS),
            whole(wd.shape),
        ],
        [by_rows(ROWS, D), by_rows(2, ROWS, WIDE)],
        [shaped(ALL_ROWS, D), shaped(2, ALL_ROWS, WIDE)],
        4_000_000_000, 30_000_000,
    )(grad_rows, row_of, weight, gate, up, wd)


def back_rows(core, own, other, wgu, lent):
    return stepped(
        back_kernel, 1, STEPS,
        [by_rows(2, ROWS, WIDE), by_rows(2, ROWS, WIDE), whole(wgu.shape), whole((2, UNITS, HALF))],
        by_rows(DEPTH, ROWS, SHARE), shaped(DEPTH, ALL_ROWS, SHARE), 4_000_000_000, 10_000_000,
    )(core, own, other, wgu, lent)


def weight_grads(core, own, other, cot, dgu, hidden):
    def block(first):
        return lambda i, c: (0, jnp.clip(i - DEPTH * (c[0] if first else 1 - c[0]), 0, DEPTH - 1))

    return stepped(
        weight_grad_kernel, 1, TENSOR,
        [
            pl.BlockSpec((ALL_ROWS, SHARE), block(True)),
            pl.BlockSpec((ALL_ROWS, SHARE), block(False)),
            pl.BlockSpec((ALL_ROWS, SHARE), lambda i, c: (0, i)),
            whole(dgu.shape),
            whole(hidden.shape),
        ],
        [
            pl.BlockSpec((2, UNITS, SHARE), lambda i, c: (0, 0, i)),
            pl.BlockSpec((UNITS, SHARE), lambda i, c: (0, i)),
        ],
        [shaped(2, UNITS, D), shaped(UNITS, D)], 6_000_000_000, 25_000_000,
    )(core, own, other, cot, dgu, hidden)


def combine(returned, own_weight):
    return pl.pallas_call(
        combine_kernel,
        in_specs=[pl.BlockSpec(memory_space=pltpu.VMEM)] * 2,
        out_shape=jax.ShapeDtypeStruct((TOK, SHARE), BF16),
        compiler_params=pltpu.CompilerParams(vmem_limit_bytes=VMEM_LIMIT),
        cost_estimate=pl.CostEstimate(flops=200_000_000, bytes_accessed=1_400_000, transcendentals=0),
    )(returned, own_weight)


def depth_parts(level, returned, own_weight, after):
    return pl.pallas_call(
        depth_kernel,
        grid_spec=pltpu.PrefetchScalarGridSpec(
            num_scalar_prefetch=1,
            grid=(DEPTH,),
            in_specs=[
                pl.BlockSpec((EXPERTS, CAP, SHARE), lambda d, z: (0, 0, (z[0] + d) % DEPTH)),
                pl.BlockSpec((TOK, EXPERTS), lambda d, z: (0, 0)),
                pl.BlockSpec(memory_space=pl.ANY),
            ],
            out_specs=pl.BlockSpec((None, TOK, SHARE), lambda d, z: (d, 0, 0)),
        ),
        out_shape=jax.ShapeDtypeStruct((DEPTH, TOK, SHARE), BF16),
        compiler_params=params(),
        cost_estimate=pl.CostEstimate(flops=90_000_000_000, bytes_accessed=5_300_000, transcendentals=0),
    )(level, returned, own_weight, after)


def over_experts(x):
    return lax.all_to_all(x, "expert", split_axis=0, concat_axis=0, tiled=True)


def swap_cores(x):
    return lax.ppermute(x, "tensor", [(t, t ^ 1) for t in range(TENSOR)])


def up_levels(x, d):
    return lax.ppermute(x, "tensor", [(t, (t + 2 * d) % TENSOR) for t in range(TENSOR)])


def on_device(tokens, expert_ids, gate_probs, grad_out, gate_up, down_proj):
    part = TOK // TENSOR
    member = lax.axis_index("tensor")
    core, level = member % 2, member // 2
    core_list, level_list = core.reshape(1).astype(jnp.int32), level.reshape(1).astype(jnp.int32)
    wgu, wd = gate_up[0], down_proj[0]

    mine = lax.dynamic_slice_in_dim(grad_out, member * part, part, 0)
    grad_rows = lax.all_gather(mine, ("expert", "tensor"), axis=0, tiled=True)

    named = expert_ids[:, :, None] == jnp.arange(EXPERTS, dtype=jnp.int32)
    own_weight = jnp.sum(jnp.where(named, gate_probs[:, :, None], 0.0), axis=1)
    weight_rows = own_weight.T
    x_half = lax.dynamic_slice_in_dim(tokens, core * HALF, HALF, 1)
    picked = pick(x_half, weight_rows)
    own_rows = over_experts(picked).reshape(ALL_ROWS, HALF)
    lent = swap_cores(lend(1 - core_list, picked, wgu, wd))
    other_rows = swap_cores(own_rows)
    weight_rows, own_rows = lax.optimization_barrier((weight_rows, own_rows))
    weight = over_experts(weight_rows)
    mask = weight > 0.0
    place = jnp.arange(TOK, dtype=jnp.int32)
    earlier = (place[:, None] < place[None, :]).astype(BF16)
    slot = jnp.dot(mask.astype(BF16), earlier, preferred_element_type=F32).astype(jnp.int32)
    offset = CAP * (jnp.arange(GROUPS, dtype=jnp.int32) % 2)
    row_of = jnp.where(mask, slot + offset[:, None], -1).reshape(GROUPS // 2, 1, 2 * TOK)
    weight = weight.reshape(GROUPS // 2, 1, 2 * TOK)

    gate, up, hidden = hidden_units(core_list, own_rows, other_rows, wgu)
    pair_out = out_rows(core_list, hidden, swap_cores(hidden), wd, lent)
    pair_out, gate = lax.optimization_barrier((pair_out, gate))
    out_back = over_experts(pair_out.reshape(GROUPS, CAP, HALF))

    cot, dgu = unit_grads(grad_rows, row_of, weight, gate, up, wd)
    pair_back = back_rows(core_list, dgu, swap_cores(dgu), wgu, lent)
    back_sum = lax.psum_scatter(
        pair_back, "tensor", scatter_dimension=0, tiled=False,
        axis_index_groups=[[2 * z + c for z in range(DEPTH)] for c in range(2)],
    )
    grad_gate_up, grad_down = weight_grads(core_list, own_rows, other_rows, cot, dgu, hidden)
    parts = depth_parts(level_list, out_back, own_weight, grad_down)
    parts, back_sum = lax.optimization_barrier((parts, back_sum))
    grad_back = over_experts(back_sum.reshape(GROUPS, CAP, SHARE))
    mixed = parts[0].astype(F32)
    for d in range(1, DEPTH):
        mixed += up_levels(parts[d], d).astype(F32)
    grad_tokens = combine(grad_back, own_weight)
    return (mixed.astype(BF16), grad_tokens, grad_gate_up[None], grad_down[None])


def solution(mesh):
    return jax.shard_map(
        on_device,
        mesh=mesh,
        in_specs=(
            P("expert", None),
            P("expert", None),
            P("expert", None),
            P("expert", None),
            P("expert", None, "tensor", None),
            P("expert", "tensor", None),
        ),
        out_specs=(
            P("expert", "tensor"),
            P("expert", "tensor"),
            P("expert", None, "tensor", None),
            P("expert", "tensor", None),
        ),
        check_vma=False,
    )
```

```python
import jax
import jax.numpy as jnp
from jax import lax
from jax.experimental import pallas as pl
from jax.experimental.pallas import tpu as pltpu
from jax.sharding import PartitionSpec as P

EXPERTS = 16
CAP = 72
GROUPS = 16
TOK = 128
D = 4096
UNITS = 192
WIDE = 256
TENSOR = 8
SHARE = D // TENSOR
HALF = D // 2
DEPTH = TENSOR // 2
STEP_GROUPS = 4
PAIRS = STEP_GROUPS // 2
ROWS = STEP_GROUPS * CAP
STEPS = GROUPS // STEP_GROUPS
ALL_ROWS = GROUPS * CAP
F32 = jnp.float32
BF16 = jnp.bfloat16
VMEM_LIMIT = 56 * 1024 * 1024


def nt(a, b):
    return lax.dot_general(a, b, (((1,), (1,)), ((), ())), preferred_element_type=F32)


def tn(a, b):
    return lax.dot_general(a, b, (((0,), (0,)), ((), ())), preferred_element_type=F32)


def nn(a, b):
    return lax.dot_general(a, b, (((1,), (0,)), ((), ())), preferred_element_type=F32)


def pick_kernel(x_ref, w_ref, o_ref):
    mask = w_ref[...] > 0.0
    earlier = lax.broadcasted_iota(jnp.int32, (TOK, TOK), 0) < lax.broadcasted_iota(jnp.int32, (TOK, TOK), 1)
    ones = jnp.where(mask, 1.0, 0.0).astype(BF16)
    slot = nn(ones, jnp.where(earlier, 1.0, 0.0).astype(BF16))
    slot = jnp.where(mask, slot, -1.0).astype(jnp.int32)
    x = x_ref[...]
    for e in range(EXPERTS):
        hit = lax.broadcasted_iota(jnp.int32, (CAP, TOK), 0) == slot[e : e + 1]
        o_ref[e] = nn(jnp.where(hit, 1.0, 0.0).astype(BF16), x).astype(BF16)


def lend_kernel(core_ref, after_ref, wgu_ref, wd_ref, o_ref):
    o_ref[0:2] = wgu_ref[...]
    o_ref[2] = wd_ref[...]


def hidden_kernel(core_ref, own_ref, other_ref, wgu_ref, gate_ref, up_ref, hid_ref):
    mine = pl.ds(pl.multiple_of(core_ref[0] * HALF, HALF), HALF)
    theirs = pl.ds(pl.multiple_of((1 - core_ref[0]) * HALF, HALF), HALF)
    own, other = own_ref[...], other_ref[...]
    gate = nt(own, wgu_ref[0, :, mine]) + nt(other, wgu_ref[0, :, theirs])
    up = nt(own, wgu_ref[1, :, mine]) + nt(other, wgu_ref[1, :, theirs])
    gate_ref[...] = gate
    up_ref[...] = up
    hid_ref[:, :UNITS] = (gate * jax.nn.sigmoid(gate) * up).astype(BF16)
    hid_ref[:, UNITS:] = jnp.zeros((ROWS, WIDE - UNITS), BF16)


def out_kernel(core_ref, own_ref, other_ref, wd_ref, lent_ref, o_ref):
    own, other = own_ref[:, :UNITS], other_ref[:, :UNITS]
    for z in range(DEPTH):
        cols = pl.ds(pl.multiple_of((2 * z + core_ref[0]) * SHARE, SHARE), SHARE)
        share = slice(SHARE * z, SHARE * (z + 1))
        o_ref[:, share] = (nn(own, wd_ref[:, cols]) + nn(other, lent_ref[:, share])).astype(BF16)


def unit_grad_kernel(g_ref, row_ref, w_ref, gate_ref, up_ref, wd_ref, cot_ref, dgu_ref):
    for j in range(PAIRS):
        g = g_ref[2 * TOK * j : 2 * TOK * (j + 1), :]
        hit = lax.broadcasted_iota(jnp.int32, (2 * CAP, 2 * TOK), 0) == row_ref[j]
        onehot = jnp.where(hit, 1.0, 0.0).astype(BF16)
        weight = jnp.sum(jnp.where(hit, w_ref[j], 0.0), axis=1, keepdims=True)
        cot_ref[2 * CAP * j : 2 * CAP * (j + 1), :] = (nn(onehot, g) * weight).astype(BF16)
    dhid = nt(cot_ref[...], wd_ref[...])
    gate = gate_ref[...]
    up = up_ref[...]
    sig = jax.nn.sigmoid(gate)
    dgu_ref[:, :, UNITS:] = jnp.zeros((2, ROWS, WIDE - UNITS), BF16)
    dgu_ref[0, :, :UNITS] = (dhid * up * sig * (1.0 + gate * (1.0 - sig))).astype(BF16)
    dgu_ref[1, :, :UNITS] = (dhid * gate * sig).astype(BF16)


def weight_grad_kernel(core_ref, after_ref, own_ref, other_ref, cot_ref, dgu_ref, hid_ref, gu_ref, down_ref):
    down_ref[...] = tn(hid_ref[:, :UNITS], cot_ref[...]).astype(BF16)
    owned = pl.program_id(0) // DEPTH == core_ref[0]

    def write(x):
        gu_ref[0] = tn(dgu_ref[0, :, :UNITS], x).astype(BF16)
        gu_ref[1] = tn(dgu_ref[1, :, :UNITS], x).astype(BF16)

    @pl.when(owned)
    def _():
        write(own_ref[...])

    @pl.when(jnp.logical_not(owned))
    def _():
        write(other_ref[...])


def back_kernel(core_ref, own_ref, other_ref, wgu_ref, lent_ref, o_ref):
    for z in range(DEPTH):
        cols = pl.ds(pl.multiple_of((2 * z + core_ref[0]) * SHARE, SHARE), SHARE)
        share = slice(SHARE * z, SHARE * (z + 1))
        total = nn(own_ref[0, :, :UNITS], wgu_ref[0, :, cols]) + nn(own_ref[1, :, :UNITS], wgu_ref[1, :, cols])
        total += nn(other_ref[0, :, :UNITS], lent_ref[0, :, share])
        total += nn(other_ref[1, :, :UNITS], lent_ref[1, :, share])
        o_ref[z] = total.astype(BF16)


def own_places(w_ref):
    w = w_ref[...]
    mask = w > 0.0
    ones = jnp.where(mask, 1.0, 0.0)
    lower = lax.broadcasted_iota(jnp.int32, (TOK, TOK), 1) < lax.broadcasted_iota(jnp.int32, (TOK, TOK), 0)
    slot = nn(jnp.where(lower, 1.0, 0.0).astype(BF16), ones.astype(BF16))
    return w, ones, jnp.where(mask, slot, -1.0).astype(jnp.int32)


def combine_kernel(r_ref, w_ref, o_ref):
    _, ones, slot = own_places(w_ref)
    total = jnp.zeros(o_ref.shape, F32)
    for e in range(EXPERTS):
        hit = lax.broadcasted_iota(jnp.int32, (TOK, CAP), 1) == slot[:, e : e + 1]
        onehot = jnp.where(hit, 1.0, 0.0).astype(BF16)
        total += nn(onehot, r_ref[e]) * ones[:, e : e + 1]
    o_ref[...] = total.astype(BF16)


def depth_kernel(z_ref, r_ref, w_ref, after_ref, o_ref):
    w, _, slot = own_places(w_ref)
    total = jnp.zeros((TOK, SHARE), F32)
    for e in range(EXPERTS):
        hit = lax.broadcasted_iota(jnp.int32, (TOK, CAP), 1) == slot[:, e : e + 1]
        onehot = jnp.where(hit, 1.0, 0.0).astype(BF16)
        total += nn(onehot, r_ref[e]) * w[:, e : e + 1]
    o_ref[...] = total.astype(BF16)


def params():
    return pltpu.CompilerParams(vmem_limit_bytes=VMEM_LIMIT, dimension_semantics=("arbitrary",))


def whole(shape):
    return pl.BlockSpec(shape, lambda *_: (0,) * len(shape), pipeline_mode=pl.Buffered(1))


def by_rows(*shape):
    return pl.BlockSpec(shape, lambda i, *_: (0,) * (len(shape) - 2) + (i, 0))


def shaped(*shape, dtype=BF16):
    return jax.ShapeDtypeStruct(shape, dtype)


def stepped(kernel, scalars, steps, in_specs, out_specs, out_shape, flops, moved):
    return pl.pallas_call(
        kernel,
        grid_spec=pltpu.PrefetchScalarGridSpec(
            num_scalar_prefetch=scalars, grid=(steps,), in_specs=in_specs, out_specs=out_specs
        ),
        out_shape=out_shape,
        compiler_params=params(),
        cost_estimate=pl.CostEstimate(flops=flops, bytes_accessed=moved, transcendentals=0),
    )


ROW_SPEC = pl.BlockSpec((PAIRS, 1, 2 * TOK), lambda i, *_: (i, 0, 0))


def pick(x_half, weight_rows):
    return pl.pallas_call(
        pick_kernel,
        out_shape=jax.ShapeDtypeStruct((EXPERTS, CAP, HALF), BF16),
        compiler_params=pltpu.CompilerParams(vmem_limit_bytes=VMEM_LIMIT),
        cost_estimate=pl.CostEstimate(flops=600_000_000, bytes_accessed=5_300_000, transcendentals=0),
    )(x_half, weight_rows)


def lend(other_core, after, wgu, wd):
    return stepped(
        lend_kernel, 1, DEPTH,
        [
            pl.BlockSpec(memory_space=pl.ANY),
            pl.BlockSpec((2, UNITS, SHARE), lambda z, c: (0, 0, 2 * z + c[0])),
            pl.BlockSpec((UNITS, SHARE), lambda z, c: (0, 2 * z + c[0])),
        ],
        pl.BlockSpec((3, UNITS, SHARE), lambda z, c: (0, 0, z)),
        shaped(3, UNITS, HALF), 0, 4_700_000,
    )(other_core, after, wgu, wd)


def hidden_units(core, own, other, wgu):
    return stepped(
        hidden_kernel, 1, STEPS,
        [by_rows(ROWS, HALF), by_rows(ROWS, HALF), whole(wgu.shape)],
        [by_rows(ROWS, UNITS), by_rows(ROWS, UNITS), by_rows(ROWS, WIDE)],
        [
            shaped(ALL_ROWS, UNITS, dtype=F32), shaped(ALL_ROWS, UNITS, dtype=F32),
            shaped(ALL_ROWS, WIDE),
        ],
        4_000_000_000, 15_000_000,
    )(core, own, other, wgu)


def out_rows(core, own, other, wd, lent):
    return stepped(
        out_kernel, 1, STEPS,
        [
            by_rows(ROWS, WIDE), by_rows(ROWS, WIDE), whole(wd.shape),
            pl.BlockSpec((None, UNITS, HALF), lambda *_: (2, 0, 0), pipeline_mode=pl.Buffered(1)),
        ],
        by_rows(ROWS, HALF), shaped(ALL_ROWS, HALF), 2_000_000_000, 8_000_000,
    )(core, own, other, wd, lent)


def unit_grads(grad_rows, row_of, weight, gate, up, wd):
    return stepped(
        unit_grad_kernel, 0, STEPS,
        [
            by_rows(STEP_GROUPS * TOK, D), ROW_SPEC, ROW_SPEC, by_rows(ROWS, UNITS), by_rows(ROWS, UNITS),
            whole(wd.shape),
        ],
        [by_rows(ROWS, D), by_rows(2, ROWS, WIDE)],
        [shaped(ALL_ROWS, D), shaped(2, ALL_ROWS, WIDE)],
        1_000_000, 100_000,
    )(grad_rows, row_of, weight, gate, up, wd)


def back_rows(core, own, other, wgu, lent):
    return stepped(
        back_kernel, 1, STEPS,
        [by_rows(2, ROWS, WIDE), by_rows(2, ROWS, WIDE), whole(wgu.shape), whole((2, UNITS, HALF))],
        by_rows(DEPTH, ROWS, SHARE), shaped(DEPTH, ALL_ROWS, SHARE), 1_000_000, 100_000,
    )(core, own, other, wgu, lent)


def weight_grads(core, after, own, other, cot, dgu, hidden):
    def block(first):
        return lambda i, c: (0, jnp.clip(i - DEPTH * (c[0] if first else 1 - c[0]), 0, DEPTH - 1))

    return stepped(
        weight_grad_kernel, 1, TENSOR,
        [
            pl.BlockSpec(memory_space=pl.ANY),
            pl.BlockSpec((ALL_ROWS, SHARE), block(True)),
            pl.BlockSpec((ALL_ROWS, SHARE), block(False)),
            pl.BlockSpec((ALL_ROWS, SHARE), lambda i, c: (0, i)),
            whole(dgu.shape),
            whole(hidden.shape),
        ],
        [
            pl.BlockSpec((2, UNITS, SHARE), lambda i, c: (0, 0, i)),
            pl.BlockSpec((UNITS, SHARE), lambda i, c: (0, i)),
        ],
        [shaped(2, UNITS, D), shaped(UNITS, D)], 6_000_000_000, 25_000_000,
    )(core, after, own, other, cot, dgu, hidden)


def combine(returned, own_weight):
    return pl.pallas_call(
        combine_kernel,
        in_specs=[pl.BlockSpec(memory_space=pltpu.VMEM)] * 2,
        out_shape=jax.ShapeDtypeStruct((TOK, SHARE), BF16),
        compiler_params=pltpu.CompilerParams(vmem_limit_bytes=VMEM_LIMIT),
        cost_estimate=pl.CostEstimate(flops=200_000_000, bytes_accessed=1_400_000, transcendentals=0),
    )(returned, own_weight)


def depth_parts(level, returned, own_weight, after):
    return pl.pallas_call(
        depth_kernel,
        grid_spec=pltpu.PrefetchScalarGridSpec(
            num_scalar_prefetch=1,
            grid=(DEPTH,),
            in_specs=[
                pl.BlockSpec((EXPERTS, CAP, SHARE), lambda d, z: (0, 0, (z[0] + d) % DEPTH)),
                pl.BlockSpec((TOK, EXPERTS), lambda d, z: (0, 0)),
                pl.BlockSpec(memory_space=pl.ANY),
            ],
            out_specs=pl.BlockSpec((None, TOK, SHARE), lambda d, z: (d, 0, 0)),
        ),
        out_shape=jax.ShapeDtypeStruct((DEPTH, TOK, SHARE), BF16),
        compiler_params=params(),
        cost_estimate=pl.CostEstimate(flops=90_000_000_000, bytes_accessed=5_300_000, transcendentals=0),
    )(level, returned, own_weight, after)


def over_experts(x):
    return lax.all_to_all(x, "expert", split_axis=0, concat_axis=0, tiled=True)


def swap_cores(x):
    return lax.ppermute(x, "tensor", [(t, t ^ 1) for t in range(TENSOR)])


def up_levels(x, d):
    return lax.ppermute(x, "tensor", [(t, (t + 2 * d) % TENSOR) for t in range(TENSOR)])


def ring_over_levels(x, level):
    half = ALL_ROWS // 2

    def block(d):
        return lax.dynamic_index_in_dim(x, (level + d) % DEPTH, 0, keepdims=False)

    def add(*terms):
        return sum(t.astype(F32) for t in terms).astype(BF16)

    far, above, below, own = block(2), block(1), block(3), block(0)
    far_up, far_down = up_levels(far[:half], 1), up_levels(far[half:], -1)
    far_up, far_down, above, below = lax.optimization_barrier((far_up, far_down, above, below))
    from_below, from_above = up_levels(above[half:], 1), up_levels(below[:half], -1)
    through_up = up_levels(add(above[:half], far_up), 1)
    through_down = up_levels(add(below[half:], far_down), -1)
    return jnp.concatenate(
        [add(own[:half], through_up, from_above), add(own[half:], from_below, through_down)], axis=0
    )


def on_device(tokens, expert_ids, gate_probs, grad_out, gate_up, down_proj):
    part = TOK // TENSOR
    member = lax.axis_index("tensor")
    core, level = member % 2, member // 2
    core_list, level_list = core.reshape(1).astype(jnp.int32), level.reshape(1).astype(jnp.int32)
    wgu, wd = gate_up[0], down_proj[0]

    mine = lax.dynamic_slice_in_dim(grad_out, member * part, part, 0)
    grad_rows = lax.all_gather(mine, ("expert", "tensor"), axis=0, tiled=True)

    named = expert_ids[:, :, None] == jnp.arange(EXPERTS, dtype=jnp.int32)
    own_weight = jnp.sum(jnp.where(named, gate_probs[:, :, None], 0.0), axis=1)
    weight_rows = own_weight.T
    x_half = lax.dynamic_slice_in_dim(tokens, core * HALF, HALF, 1)
    picked = pick(x_half, weight_rows)
    own_rows = over_experts(picked).reshape(ALL_ROWS, HALF)
    lent = swap_cores(lend(1 - core_list, picked, wgu, wd))
    other_rows = swap_cores(own_rows)
    weight_rows, own_rows = lax.optimization_barrier((weight_rows, own_rows))
    weight = over_experts(weight_rows)
    mask = weight > 0.0
    place = jnp.arange(TOK, dtype=jnp.int32)
    earlier = (place[:, None] < place[None, :]).astype(BF16)
    slot = jnp.dot(mask.astype(BF16), earlier, preferred_element_type=F32).astype(jnp.int32)
    offset = CAP * (jnp.arange(GROUPS, dtype=jnp.int32) % 2)
    row_of = jnp.where(mask, slot + offset[:, None], -1).reshape(GROUPS // 2, 1, 2 * TOK)
    weight = weight.reshape(GROUPS // 2, 1, 2 * TOK)

    gate, up, hidden = hidden_units(core_list, own_rows, other_rows, wgu)
    pair_out = out_rows(core_list, hidden, swap_cores(hidden), wd, lent)
    pair_out, gate = lax.optimization_barrier((pair_out, gate))
    out_back = over_experts(pair_out.reshape(GROUPS, CAP, HALF))

    cot, dgu = unit_grads(grad_rows, row_of, weight, gate, up, wd)
    pair_back = back_rows(core_list, dgu, swap_cores(dgu), wgu, lent)
    grad_gate_up, grad_down = weight_grads(core_list, pair_back, own_rows, other_rows, cot, dgu, hidden)
    back_sum = ring_over_levels(pair_back, level)
    back_sum, grad_down = lax.optimization_barrier((back_sum, grad_down))
    parts = depth_parts(level_list, out_back, own_weight, back_sum)
    grad_back = over_experts(back_sum.reshape(GROUPS, CAP, SHARE))
    mixed = parts[0].astype(F32)
    for d in range(1, DEPTH):
        mixed += up_levels(parts[d], d).astype(F32)
    grad_tokens = combine(grad_back, own_weight)
    return (mixed.astype(BF16), grad_tokens, grad_gate_up[None], grad_down[None])


def solution(mesh):
    return jax.shard_map(
        on_device,
        mesh=mesh,
        in_specs=(
            P("expert", None),
            P("expert", None),
            P("expert", None),
            P("expert", None),
            P("expert", None, "tensor", None),
            P("expert", "tensor", None),
        ),
        out_specs=(
            P("expert", "tensor"),
            P("expert", "tensor"),
            P("expert", None, "tensor", None),
            P("expert", "tensor", None),
        ),
        check_vma=False,
    )
```

```python
import jax
import jax.numpy as jnp
from jax import lax
from jax.experimental import pallas as pl
from jax.experimental.pallas import tpu as pltpu
from jax.sharding import PartitionSpec as P

EXPERTS = 16
CAP = 72
GROUPS = 16
TOK = 128
D = 4096
UNITS = 192
WIDE = 256
TENSOR = 8
SHARE = D // TENSOR
HALF = D // 2
DEPTH = TENSOR // 2
STEP_GROUPS = 4
PAIRS = STEP_GROUPS // 2
ROWS = STEP_GROUPS * CAP
STEPS = GROUPS // STEP_GROUPS
ALL_ROWS = GROUPS * CAP
F32 = jnp.float32
BF16 = jnp.bfloat16
VMEM_LIMIT = 56 * 1024 * 1024


def nt(a, b):
    return lax.dot_general(a, b, (((1,), (1,)), ((), ())), preferred_element_type=F32)


def tn(a, b):
    return lax.dot_general(a, b, (((0,), (0,)), ((), ())), preferred_element_type=F32)


def nn(a, b):
    return lax.dot_general(a, b, (((1,), (0,)), ((), ())), preferred_element_type=F32)


def pick_kernel(x_ref, w_ref, o_ref):
    mask = w_ref[...] > 0.0
    earlier = lax.broadcasted_iota(jnp.int32, (TOK, TOK), 0) < lax.broadcasted_iota(jnp.int32, (TOK, TOK), 1)
    ones = jnp.where(mask, 1.0, 0.0).astype(BF16)
    slot = nn(ones, jnp.where(earlier, 1.0, 0.0).astype(BF16))
    slot = jnp.where(mask, slot, -1.0).astype(jnp.int32)
    x = x_ref[...]
    for e in range(EXPERTS):
        hit = lax.broadcasted_iota(jnp.int32, (CAP, TOK), 0) == slot[e : e + 1]
        o_ref[e] = nn(jnp.where(hit, 1.0, 0.0).astype(BF16), x).astype(BF16)


def lend_kernel(core_ref, after_ref, wgu_ref, wd_ref, o_ref):
    o_ref[0:2] = wgu_ref[...]
    o_ref[2] = wd_ref[...]


def hidden_kernel(core_ref, own_ref, other_ref, wgu_ref, gate_ref, up_ref, hid_ref):
    mine = pl.ds(pl.multiple_of(core_ref[0] * HALF, HALF), HALF)
    theirs = pl.ds(pl.multiple_of((1 - core_ref[0]) * HALF, HALF), HALF)
    own, other = own_ref[...], other_ref[...]
    gate = nt(own, wgu_ref[0, :, mine]) + nt(other, wgu_ref[0, :, theirs])
    up = nt(own, wgu_ref[1, :, mine]) + nt(other, wgu_ref[1, :, theirs])
    gate_ref[...] = gate
    up_ref[...] = up
    hid_ref[:, :UNITS] = (gate * jax.nn.sigmoid(gate) * up).astype(BF16)
    hid_ref[:, UNITS:] = jnp.zeros((ROWS, WIDE - UNITS), BF16)


def out_kernel(core_ref, own_ref, other_ref, wd_ref, lent_ref, o_ref):
    own, other = own_ref[:, :UNITS], other_ref[:, :UNITS]
    for z in range(DEPTH):
        cols = pl.ds(pl.multiple_of((2 * z + core_ref[0]) * SHARE, SHARE), SHARE)
        share = slice(SHARE * z, SHARE * (z + 1))
        o_ref[:, share] = (nn(own, wd_ref[:, cols]) + nn(other, lent_ref[:, share])).astype(BF16)


def unit_grad_kernel(g_ref, row_ref, w_ref, gate_ref, up_ref, wd_ref, cot_ref, dgu_ref):
    for j in range(PAIRS):
        g = g_ref[2 * TOK * j : 2 * TOK * (j + 1), :]
        hit = lax.broadcasted_iota(jnp.int32, (2 * CAP, 2 * TOK), 0) == row_ref[j]
        onehot = jnp.where(hit, 1.0, 0.0).astype(BF16)
        weight = jnp.sum(jnp.where(hit, w_ref[j], 0.0), axis=1, keepdims=True)
        cot_ref[2 * CAP * j : 2 * CAP * (j + 1), :] = (nn(onehot, g) * weight).astype(BF16)
    dhid = nt(cot_ref[...], wd_ref[...])
    gate = gate_ref[...]
    up = up_ref[...]
    sig = jax.nn.sigmoid(gate)
    dgu_ref[:, :, UNITS:] = jnp.zeros((2, ROWS, WIDE - UNITS), BF16)
    dgu_ref[0, :, :UNITS] = (dhid * up * sig * (1.0 + gate * (1.0 - sig))).astype(BF16)
    dgu_ref[1, :, :UNITS] = (dhid * gate * sig).astype(BF16)


def weight_grad_kernel(core_ref, after_ref, own_ref, other_ref, cot_ref, dgu_ref, hid_ref, gu_ref, down_ref):
    down_ref[...] = tn(hid_ref[:, :UNITS], cot_ref[...]).astype(BF16)
    owned = pl.program_id(0) // DEPTH == core_ref[0]

    def write(x):
        gu_ref[0] = tn(dgu_ref[0, :, :UNITS], x).astype(BF16)
        gu_ref[1] = tn(dgu_ref[1, :, :UNITS], x).astype(BF16)

    @pl.when(owned)
    def _():
        write(own_ref[...])

    @pl.when(jnp.logical_not(owned))
    def _():
        write(other_ref[...])


def back_kernel(core_ref, own_ref, other_ref, wgu_ref, lent_ref, o_ref):
    for z in range(DEPTH):
        cols = pl.ds(pl.multiple_of((2 * z + core_ref[0]) * SHARE, SHARE), SHARE)
        share = slice(SHARE * z, SHARE * (z + 1))
        total = nn(own_ref[0, :, :UNITS], wgu_ref[0, :, cols]) + nn(own_ref[1, :, :UNITS], wgu_ref[1, :, cols])
        total += nn(other_ref[0, :, :UNITS], lent_ref[0, :, share])
        total += nn(other_ref[1, :, :UNITS], lent_ref[1, :, share])
        o_ref[z] = total.astype(BF16)


def own_places(w_ref):
    w = w_ref[...]
    mask = w > 0.0
    ones = jnp.where(mask, 1.0, 0.0)
    lower = lax.broadcasted_iota(jnp.int32, (TOK, TOK), 1) < lax.broadcasted_iota(jnp.int32, (TOK, TOK), 0)
    slot = nn(jnp.where(lower, 1.0, 0.0).astype(BF16), ones.astype(BF16))
    return w, ones, jnp.where(mask, slot, -1.0).astype(jnp.int32)


def combine_kernel(r_ref, w_ref, o_ref):
    _, ones, slot = own_places(w_ref)
    total = jnp.zeros(o_ref.shape, F32)
    for e in range(EXPERTS):
        hit = lax.broadcasted_iota(jnp.int32, (TOK, CAP), 1) == slot[:, e : e + 1]
        onehot = jnp.where(hit, 1.0, 0.0).astype(BF16)
        total += nn(onehot, r_ref[e]) * ones[:, e : e + 1]
    o_ref[...] = total.astype(BF16)


def depth_kernel(z_ref, r_ref, w_ref, after_ref, o_ref):
    w, _, slot = own_places(w_ref)
    total = jnp.zeros((TOK, SHARE), F32)
    for e in range(EXPERTS):
        hit = lax.broadcasted_iota(jnp.int32, (TOK, CAP), 1) == slot[:, e : e + 1]
        onehot = jnp.where(hit, 1.0, 0.0).astype(BF16)
        total += nn(onehot, r_ref[e]) * w[:, e : e + 1]
    o_ref[...] = total.astype(BF16)


def params():
    return pltpu.CompilerParams(vmem_limit_bytes=VMEM_LIMIT, dimension_semantics=("arbitrary",))


def whole(shape):
    return pl.BlockSpec(shape, lambda *_: (0,) * len(shape), pipeline_mode=pl.Buffered(1))


def by_rows(*shape):
    return pl.BlockSpec(shape, lambda i, *_: (0,) * (len(shape) - 2) + (i, 0))


def shaped(*shape, dtype=BF16):
    return jax.ShapeDtypeStruct(shape, dtype)


def stepped(kernel, scalars, steps, in_specs, out_specs, out_shape, flops, moved):
    return pl.pallas_call(
        kernel,
        grid_spec=pltpu.PrefetchScalarGridSpec(
            num_scalar_prefetch=scalars, grid=(steps,), in_specs=in_specs, out_specs=out_specs
        ),
        out_shape=out_shape,
        compiler_params=params(),
        cost_estimate=pl.CostEstimate(flops=flops, bytes_accessed=moved, transcendentals=0),
    )


ROW_SPEC = pl.BlockSpec((PAIRS, 1, 2 * TOK), lambda i, *_: (i, 0, 0))


def pick(x_half, weight_rows):
    return pl.pallas_call(
        pick_kernel,
        out_shape=jax.ShapeDtypeStruct((EXPERTS, CAP, HALF), BF16),
        compiler_params=pltpu.CompilerParams(vmem_limit_bytes=VMEM_LIMIT),
        cost_estimate=pl.CostEstimate(flops=600_000_000, bytes_accessed=5_300_000, transcendentals=0),
    )(x_half, weight_rows)


def lend(other_core, after, wgu, wd):
    return stepped(
        lend_kernel, 1, DEPTH,
        [
            pl.BlockSpec(memory_space=pl.ANY),
            pl.BlockSpec((2, UNITS, SHARE), lambda z, c: (0, 0, 2 * z + c[0])),
            pl.BlockSpec((UNITS, SHARE), lambda z, c: (0, 2 * z + c[0])),
        ],
        pl.BlockSpec((3, UNITS, SHARE), lambda z, c: (0, 0, z)),
        shaped(3, UNITS, HALF), 0, 4_700_000,
    )(other_core, after, wgu, wd)


def hidden_units(core, own, other, wgu):
    return stepped(
        hidden_kernel, 1, STEPS,
        [by_rows(ROWS, HALF), by_rows(ROWS, HALF), whole(wgu.shape)],
        [by_rows(ROWS, UNITS), by_rows(ROWS, UNITS), by_rows(ROWS, WIDE)],
        [
            shaped(ALL_ROWS, UNITS, dtype=F32), shaped(ALL_ROWS, UNITS, dtype=F32),
            shaped(ALL_ROWS, WIDE),
        ],
        4_000_000_000, 15_000_000,
    )(core, own, other, wgu)


def out_rows(core, own, other, wd, lent):
    return stepped(
        out_kernel, 1, STEPS,
        [
            by_rows(ROWS, WIDE), by_rows(ROWS, WIDE), whole(wd.shape),
            pl.BlockSpec((None, UNITS, HALF), lambda *_: (2, 0, 0), pipeline_mode=pl.Buffered(1)),
        ],
        by_rows(ROWS, HALF), shaped(ALL_ROWS, HALF), 2_000_000_000, 8_000_000,
    )(core, own, other, wd, lent)


def unit_grads(grad_rows, row_of, weight, gate, up, wd):
    return stepped(
        unit_grad_kernel, 0, STEPS,
        [
            by_rows(STEP_GROUPS * TOK, D), ROW_SPEC, ROW_SPEC, by_rows(ROWS, UNITS), by_rows(ROWS, UNITS),
            whole(wd.shape),
        ],
        [by_rows(ROWS, D), by_rows(2, ROWS, WIDE)],
        [shaped(ALL_ROWS, D), shaped(2, ALL_ROWS, WIDE)],
        1_000_000, 100_000,
    )(grad_rows, row_of, weight, gate, up, wd)


def back_rows(core, own, other, wgu, lent):
    return stepped(
        back_kernel, 1, STEPS,
        [by_rows(2, ROWS, WIDE), by_rows(2, ROWS, WIDE), whole(wgu.shape), whole((2, UNITS, HALF))],
        by_rows(DEPTH, ROWS, SHARE), shaped(DEPTH, ALL_ROWS, SHARE), 1_000_000, 100_000,
    )(core, own, other, wgu, lent)


def weight_grads(core, after, own, other, cot, dgu, hidden):
    def block(first):
        return lambda i, c: (0, jnp.clip(i - DEPTH * (c[0] if first else 1 - c[0]), 0, DEPTH - 1))

    return stepped(
        weight_grad_kernel, 1, TENSOR,
        [
            pl.BlockSpec(memory_space=pl.ANY),
            pl.BlockSpec((ALL_ROWS, SHARE), block(True)),
            pl.BlockSpec((ALL_ROWS, SHARE), block(False)),
            pl.BlockSpec((ALL_ROWS, SHARE), lambda i, c: (0, i)),
            whole(dgu.shape),
            whole(hidden.shape),
        ],
        [
            pl.BlockSpec((2, UNITS, SHARE), lambda i, c: (0, 0, i)),
            pl.BlockSpec((UNITS, SHARE), lambda i, c: (0, i)),
        ],
        [shaped(2, UNITS, D), shaped(UNITS, D)], 6_000_000_000, 25_000_000,
    )(core, after, own, other, cot, dgu, hidden)


def combine(returned, own_weight):
    return pl.pallas_call(
        combine_kernel,
        in_specs=[pl.BlockSpec(memory_space=pltpu.VMEM)] * 2,
        out_shape=jax.ShapeDtypeStruct((TOK, SHARE), BF16),
        compiler_params=pltpu.CompilerParams(vmem_limit_bytes=VMEM_LIMIT),
        cost_estimate=pl.CostEstimate(flops=200_000_000, bytes_accessed=1_400_000, transcendentals=0),
    )(returned, own_weight)


def depth_parts(level, returned, own_weight, after):
    return pl.pallas_call(
        depth_kernel,
        grid_spec=pltpu.PrefetchScalarGridSpec(
            num_scalar_prefetch=1,
            grid=(DEPTH,),
            in_specs=[
                pl.BlockSpec((EXPERTS, CAP, SHARE), lambda d, z: (0, 0, (z[0] + d) % DEPTH)),
                pl.BlockSpec((TOK, EXPERTS), lambda d, z: (0, 0)),
                pl.BlockSpec(memory_space=pl.ANY),
            ],
            out_specs=pl.BlockSpec((None, TOK, SHARE), lambda d, z: (d, 0, 0)),
        ),
        out_shape=jax.ShapeDtypeStruct((DEPTH, TOK, SHARE), BF16),
        compiler_params=params(),
        cost_estimate=pl.CostEstimate(flops=90_000_000_000, bytes_accessed=5_300_000, transcendentals=0),
    )(level, returned, own_weight, after)


def over_experts(x):
    return lax.all_to_all(x, "expert", split_axis=0, concat_axis=0, tiled=True)


def swap_cores(x):
    return lax.ppermute(x, "tensor", [(t, t ^ 1) for t in range(TENSOR)])


def up_levels(x, d):
    return lax.ppermute(x, "tensor", [(t, (t + 2 * d) % TENSOR) for t in range(TENSOR)])


def ring_over_levels(x, level):
    half = ALL_ROWS // 2

    def block(d):
        return lax.dynamic_index_in_dim(x, (level + d) % DEPTH, 0, keepdims=False)

    def add(*terms):
        return sum(t.astype(F32) for t in terms).astype(BF16)

    far, above, below, own = lax.optimization_barrier((block(2), block(1), block(3), block(0)))
    far_up, far_down = up_levels(far[:half], 1), up_levels(far[half:], -1)
    from_below, from_above = up_levels(above[half:], 1), up_levels(below[:half], -1)
    far_up, far_down = lax.optimization_barrier((far_up, far_down))
    through_up = up_levels(add(above[:half], far_up), 1)
    through_down = up_levels(add(below[half:], far_down), -1)
    return jnp.concatenate(
        [add(own[:half], through_up, from_above), add(own[half:], from_below, through_down)], axis=0
    )


def on_device(tokens, expert_ids, gate_probs, grad_out, gate_up, down_proj):
    part = TOK // TENSOR
    member = lax.axis_index("tensor")
    core, level = member % 2, member // 2
    core_list, level_list = core.reshape(1).astype(jnp.int32), level.reshape(1).astype(jnp.int32)
    wgu, wd = gate_up[0], down_proj[0]

    mine = lax.dynamic_slice_in_dim(grad_out, member * part, part, 0)
    grad_rows = lax.all_gather(mine, ("expert", "tensor"), axis=0, tiled=True)

    named = expert_ids[:, :, None] == jnp.arange(EXPERTS, dtype=jnp.int32)
    own_weight = jnp.sum(jnp.where(named, gate_probs[:, :, None], 0.0), axis=1)
    weight_rows = own_weight.T
    x_half = lax.dynamic_slice_in_dim(tokens, core * HALF, HALF, 1)
    picked = pick(x_half, weight_rows)
    own_rows = over_experts(picked).reshape(ALL_ROWS, HALF)
    lent = swap_cores(lend(1 - core_list, picked, wgu, wd))
    other_rows = swap_cores(own_rows)
    weight_rows, own_rows = lax.optimization_barrier((weight_rows, own_rows))
    weight = over_experts(weight_rows)
    mask = weight > 0.0
    place = jnp.arange(TOK, dtype=jnp.int32)
    earlier = (place[:, None] < place[None, :]).astype(BF16)
    slot = jnp.dot(mask.astype(BF16), earlier, preferred_element_type=F32).astype(jnp.int32)
    offset = CAP * (jnp.arange(GROUPS, dtype=jnp.int32) % 2)
    row_of = jnp.where(mask, slot + offset[:, None], -1).reshape(GROUPS // 2, 1, 2 * TOK)
    weight = weight.reshape(GROUPS // 2, 1, 2 * TOK)

    gate, up, hidden = hidden_units(core_list, own_rows, other_rows, wgu)
    pair_out = out_rows(core_list, hidden, swap_cores(hidden), wd, lent)
    pair_out, gate = lax.optimization_barrier((pair_out, gate))
    out_back = over_experts(pair_out.reshape(GROUPS, CAP, HALF))

    cot, dgu = unit_grads(grad_rows, row_of, weight, gate, up, wd)
    pair_back = back_rows(core_list, dgu, swap_cores(dgu), wgu, lent)
    grad_gate_up, grad_down = weight_grads(core_list, pair_back, own_rows, other_rows, cot, dgu, hidden)
    back_sum = ring_over_levels(pair_back, level)
    back_sum, grad_down = lax.optimization_barrier((back_sum, grad_down))
    parts = depth_parts(level_list, out_back, own_weight, back_sum)
    grad_back = over_experts(back_sum.reshape(GROUPS, CAP, SHARE))
    mixed = parts[0].astype(F32)
    for d in range(1, DEPTH):
        mixed += up_levels(parts[d], d).astype(F32)
    grad_tokens = combine(grad_back, own_weight)
    return (mixed.astype(BF16), grad_tokens, grad_gate_up[None], grad_down[None])


def solution(mesh):
    return jax.shard_map(
        on_device,
        mesh=mesh,
        in_specs=(
            P("expert", None),
            P("expert", None),
            P("expert", None),
            P("expert", None),
            P("expert", None, "tensor", None),
            P("expert", "tensor", None),
        ),
        out_specs=(
            P("expert", "tensor"),
            P("expert", "tensor"),
            P("expert", None, "tensor", None),
            P("expert", "tensor", None),
        ),
        check_vma=False,
    )
```
